32 devices in a mesh: blk: 16 (over z, x, core), rep: 2 (over y).
Axes of the slice: x: 2, y: 2, z: 4, core: 2. Of those that a mesh axis runs over, the one named last changes fastest.
Arguments:
- tokens: int32 [8192, 69], P('blk'), may hold values from 0 to 63
- lengths: int32 [8192], P('blk'), may hold values from 16 to 69
- embed: bfloat16 [64, 256], replicated, may hold values from -6 to 6
- conv_w: bfloat16 [7, 32, 256], replicated, may hold values from -0.375 to 0.375
- conv_b: float32 [256], replicated, may hold values from -3 to 3
- inv_len: float32 [256], replicated, may hold values from 0.05 to 0.3
- hyper: float32 [2], replicated, may hold values from 0.5 to 2
- probes: bfloat16 [8192, 64], P('blk'), may hold values from -6 to 6
- prev_probes: bfloat16 [8192, 64], P(('blk', 'rep')), may hold values from -6 to 6
- coupling: float32 [64, 64], replicated, may hold values from -12 to 12
Outputs:
- block_a: float32 [64, 64], replicated
- block_r: float32 [64, 64], replicated
- next_probes: float32 [8192, 64], P(('blk', 'rep'))
The draws below stay inside these ranges and needn't reach their ends.
All inputs are finite; a program needn't handle non-finite values.
Results may differ from the reference program's by a relative error of at most 0.0065.
Values may be sent and summed in bfloat16 or wider, within the bound.
A program may use at most 128 MiB of HBM per device.

```python
import math
import jax
import jax.numpy as jnp
import numpy as np
from jax import lax

CH = 256
KW = 7
SEQ = 69
VOCAB = 64
PROBES = 64
NS = 8192
GSIZE = 32
TOUT = 32


def set_ends(result, key, least, largest):
    shape = result.shape
    spot = [jax.random.randint(jax.random.fold_in(key, axis), (), 0, shape[axis]) for axis in range(len(shape))]
    result = result.at[tuple(spot)].set(least)
    longest = shape.index(max(shape))
    spot[longest] = (spot[longest] + 1) % shape[longest]
    return result.at[tuple(spot)].set(largest)


def block_scale(key, shape, shards, least, largest):
    gain, own = 1.0, jax.random.fold_in(key, 6)
    for axis_at, parts in shards:
        steps = jnp.exp(jax.random.uniform(jax.random.fold_in(own, axis_at), (parts,), jnp.float32, least / len(shards), largest / len(shards)))
        gain = gain * jnp.repeat(steps, shape[axis_at] // parts).reshape([-1 if axis == axis_at else 1 for axis in range(len(shape))])
    return gain


def rank_bounds(number_of, lean):
    weights = [(1 << 20) // math.isqrt(standing ** lean) + 1 for standing in range(1, number_of + 1)]
    scale = 1 + sum(weights) // (1 << 30)
    return np.cumsum(np.array([max(1, weight // scale) for weight in weights]))


def ranked(key, extent, amount, slope):
    listing = rank_bounds(amount, slope)
    lot = jax.random.randint(jax.random.fold_in(key, 1), extent, 0, int(listing[amount - 1]))
    rank = jnp.searchsorted(jnp.asarray(listing, jnp.int32), lot, side="right")
    return jax.random.permutation(jax.random.fold_in(key, 2), amount)[rank].astype(jnp.int32)


def bell_draw(stream_key, dims, scale, bound, cuts=(), kind=jnp.bfloat16):
    gain = block_scale(stream_key, dims, cuts, -0.22, 0.18) if cuts else 1.0
    entries = jax.random.normal(stream_key, dims, jnp.float32) * scale * gain
    return jnp.minimum(jnp.maximum(entries, -bound), bound).astype(kind)


def setup_inputs(seed: int = 0) -> dict:
    seeds = jax.random.split(jax.random.key(seed), 11)
    return {
        "tokens": set_ends(ranked(seeds[0], (NS, SEQ), VOCAB, 2), jax.random.fold_in(seeds[0], 3), 0, VOCAB - 1).astype(jnp.int32),
        "lengths": set_ends(jax.random.randint(seeds[1], (NS,), 16, SEQ + 1), jax.random.fold_in(seeds[1], 1), 16, SEQ).astype(jnp.int32),
        "embed": bell_draw(seeds[2], (VOCAB, CH), 1.0, 6.0),
        "conv_w": bell_draw(seeds[3], (KW, GSIZE, CH), (KW * GSIZE) ** -0.5, 0.375),
        "conv_b": bell_draw(seeds[4], (CH,), 0.5, 3.0, (), jnp.float32),
        "inv_len": jnp.clip(jnp.exp(jax.random.uniform(seeds[5], (CH,), jnp.float32, math.log(0.05), math.log(0.3))), 0.05, 0.3),
        "hyper": jnp.clip(jax.random.uniform(seeds[6], (2,), jnp.float32, 0.5, 2.0), 0.5, 2.0),
        "probes": bell_draw(seeds[7], (NS, PROBES), 1.0, 6.0, ((0, 16),)),
        "prev_probes": bell_draw(seeds[8], (NS, PROBES), 1.0, 6.0, ((0, 32),)),
        "coupling": bell_draw(seeds[9], (PROBES, PROBES), 2.0, 12.0, (), jnp.float32),
    }


def upper_factor(gram):
    order = gram.shape[0]
    index_row = jnp.arange(order, dtype=jnp.int32)

    def column_step(column, carry):
        work, lower = carry
        pivot = lax.dynamic_slice(work, (column, column), (1, 1))[0, 0]
        vector = lax.dynamic_slice_in_dim(work, column, 1, 1)[:, 0]
        vector = jnp.where(index_row >= column, vector * lax.rsqrt(pivot), 0.0)
        lower = lower + vector[:, None] * (index_row == column).astype(jnp.float32)[None, :]
        work = work - vector[:, None] * vector[None, :]
        return (work, lower)
    _, lower = lax.fori_loop(0, order, column_step, (gram, jnp.zeros_like(gram)))
    return lower.T

def upper_inverse(upper):
    order = upper.shape[0]
    index_row = jnp.arange(order, dtype=jnp.int32)

    def row_step(count, solved):
        row = order - 1 - count
        upper_row = lax.dynamic_slice_in_dim(upper, row, 1, 0)
        diag_value = lax.dynamic_slice(upper, (row, row), (1, 1))[0, 0]
        unit_row = (index_row == row).astype(jnp.float32)[None, :]
        product = jnp.dot(upper_row, solved, precision=lax.Precision.HIGHEST, preferred_element_type=jnp.float32)
        new_row = (unit_row - product) / diag_value
        return solved + (index_row == row).astype(jnp.float32)[:, None] * new_row
    return lax.fori_loop(0, order, row_step, jnp.zeros_like(upper))

def features_block(tok_block, len_block, embed, conv_w, conv_b, inv_len):
    block_rows = tok_block.shape[0]
    group_count = CH // GSIZE
    embedded = jnp.take(embed, tok_block, axis=0).astype(jnp.float32)
    running = jnp.zeros((block_rows, TOUT, group_count, GSIZE), jnp.float32)
    for tap_index in range(KW):
        window = lax.slice(embedded, (0, tap_index, 0), (block_rows, tap_index + 2 * (TOUT - 1) + 1, CH), (1, 2, 1))
        window = window.reshape(block_rows, TOUT, group_count, GSIZE)
        kernel_tap = conv_w[tap_index].astype(jnp.float32).reshape(GSIZE, group_count, GSIZE)
        running = running + jnp.einsum('btgi,igo->btgo', window, kernel_tap, preferred_element_type=jnp.float32)
    preact = running.reshape(block_rows, TOUT, CH) + conv_b
    counts = (len_block - KW) // 2 + 1
    valid_mask = (jnp.arange(TOUT, dtype=jnp.int32)[None, :] < counts[:, None]).astype(jnp.float32)
    activated = jax.nn.gelu(preact, approximate=True) * valid_mask[:, :, None]
    pooled = lax.optimization_barrier(jnp.sum(activated, axis=1)) / counts.astype(jnp.float32)[:, None]
    row_mean = lax.optimization_barrier(jnp.mean(pooled, axis=1, keepdims=True))
    centered = pooled - row_mean
    row_var = lax.optimization_barrier(jnp.mean(centered * centered, axis=1, keepdims=True))
    normed = centered * lax.rsqrt(row_var + 1e-05)
    return (normed * inv_len).astype(jnp.bfloat16)

def reference(tokens, lengths, embed, conv_w, conv_b, inv_len, hyper, probes, prev_probes, coupling):
    block_rows = math.gcd(NS, 256)
    block_count = NS // block_rows

    def feature_step(pair):
        return features_block(pair[0], pair[1], embed, conv_w, conv_b, inv_len)
    feat = lax.map(feature_step, (tokens.reshape(block_count, block_rows, SEQ), lengths.reshape(block_count, block_rows)))
    feat = feat.reshape(NS, CH)
    feat_wide = lax.optimization_barrier(feat).astype(jnp.float32)
    sq_all = lax.optimization_barrier(jnp.sum(feat_wide * feat_wide, axis=1))
    probes_wide = probes.astype(jnp.float32)
    amplitude = hyper[0]
    noise_var = hyper[1]
    kern_rows = math.gcd(NS, 512)
    kern_count = NS // kern_rows

    def kernel_rows(pair):
        rows_feat, rows_sq = pair
        inner_prod = jnp.dot(rows_feat, feat_wide.T, preferred_element_type=jnp.float32)
        distance = jnp.maximum(rows_sq[:, None] + sq_all[None, :] - 2.0 * inner_prod, 0.0)
        weights = (amplitude * jnp.exp(-0.5 * distance)).astype(jnp.bfloat16)
        weights = lax.optimization_barrier(weights).astype(jnp.float32)
        return jnp.dot(weights, probes_wide, preferred_element_type=jnp.float32)
    applied = lax.map(kernel_rows, (feat_wide.reshape(kern_count, kern_rows, CH), sq_all.reshape(kern_count, kern_rows)))
    applied = applied.reshape(NS, PROBES) + noise_var * probes_wide
    inv_root = 1.0 / math.sqrt(NS)
    basis = probes_wide * inv_root
    coupled = jnp.dot(prev_probes.astype(jnp.float32), coupling.T, precision=lax.Precision.HIGHEST, preferred_element_type=jnp.float32) * inv_root
    image = applied * inv_root - coupled
    block_a = jnp.dot(basis.T, image, precision=lax.Precision.HIGHEST, preferred_element_type=jnp.float32)
    resid = image - jnp.dot(basis, block_a, precision=lax.Precision.HIGHEST, preferred_element_type=jnp.float32)
    gram = jnp.dot(resid.T, resid, precision=lax.Precision.HIGHEST, preferred_element_type=jnp.float32)
    upper = upper_factor(gram)
    inverse = upper_inverse(upper)
    next_probes = jnp.dot(resid, inverse, precision=lax.Precision.HIGHEST, preferred_element_type=jnp.float32) * math.sqrt(NS)
    return (block_a, upper, next_probes)
```

```python
import functools
import math

import jax
import jax.numpy as jnp
from jax import lax
from jax.experimental import pallas as pl
from jax.experimental.pallas import tpu as pltpu
from jax.sharding import PartitionSpec as P

F32 = jnp.float32
BF16 = jnp.bfloat16
EXTRA = 16
HIGH = lax.Precision.HIGHEST


def build_table(embed_ref, conv_w_ref, conv_b_ref, table, table_hi, table_lo):
    taps, width, channels = conv_w_ref.shape
    vocab = embed_ref.shape[0]
    groups = channels // width
    in_group = lax.broadcasted_iota(jnp.int32, (channels, channels), 0) // width
    out_group = lax.broadcasted_iota(jnp.int32, (channels, channels), 1) // width
    same = in_group == out_group
    for tap in range(taps):
        tiled = jnp.concatenate([conv_w_ref[tap].astype(F32)] * groups, axis=0)
        dense = jnp.where(same, tiled, 0.0).astype(BF16)
        entry = jnp.dot(embed_ref[...], dense, preferred_element_type=F32)
        if tap == 0:
            entry = entry + conv_b_ref[...]
        table[tap * vocab : (tap + 1) * vocab, :] = entry
    full = table[...].T
    high = full.astype(BF16)
    table_hi[...] = high
    table_lo[...] = (full - high.astype(F32)).astype(BF16)


def pooled_features(
    tokens_ref, lengths_ref, inv_len_ref, first, rows, taps, vocab, padded, onehot, table_hi, table_lo, pooled
):
    seq = tokens_ref.shape[1]
    channels = inv_len_ref.shape[0]
    positions = (seq - taps) // 2 + 1
    padded[...] = jnp.zeros_like(padded)
    padded[:, :seq] = tokens_ref[pl.ds(first, rows), :]
    token_rows = padded[...].T
    vocab_ids = lax.broadcasted_iota(jnp.int32, (vocab, rows), 0)
    for spot in range(seq):
        hit = jnp.broadcast_to(token_rows[spot : spot + 1, :], (vocab, rows)) == vocab_ids
        onehot[spot * vocab : (spot + 1) * vocab, :] = jnp.where(hit, 1.0, 0.0).astype(BF16)
    counts = (lengths_ref[:, pl.ds(first, rows)] - taps) // 2 + 1
    pooled[...] = jnp.zeros_like(pooled)
    root = math.sqrt(2.0 / math.pi)

    def position_step(position, carry):
        start = pl.multiple_of(position * (2 * vocab), 2 * vocab)
        window = onehot[pl.ds(start, taps * vocab), :]
        preact = jnp.dot(table_hi[...], window, preferred_element_type=F32)
        preact = preact + jnp.dot(table_lo[...], window, preferred_element_type=F32)
        inner = preact * (root + (root * 0.044715) * (preact * preact))
        half = jnp.where(position < counts, 0.5, 0.0)
        weighted = preact * half
        pooled[...] += weighted + weighted * jnp.tanh(inner)
        return carry

    lax.fori_loop(0, positions, position_step, 0)
    mean_pool = pooled[...] / counts.astype(F32)
    centered = mean_pool - jnp.mean(mean_pool, axis=0, keepdims=True)
    variance = jnp.mean(centered * centered, axis=0, keepdims=True)
    normed = centered * lax.rsqrt(variance + 1e-05)
    return (normed * inv_len_ref[...]).astype(BF16)


def feature_kernel(
    tokens_ref,
    lengths_ref,
    embed_ref,
    conv_w_ref,
    conv_b_ref,
    inv_len_ref,
    cols_ref,
    rows_ref,
    padded,
    onehot,
    table,
    table_hi,
    table_lo,
    pooled,
):
    rows = cols_ref.shape[1]
    channels = inv_len_ref.shape[0]
    first = pl.multiple_of(lax.axis_index("rep") * rows, rows)
    build_table(embed_ref, conv_w_ref, conv_b_ref, table, table_hi, table_lo)
    feat = pooled_features(
        tokens_ref,
        lengths_ref,
        inv_len_ref,
        first,
        rows,
        conv_w_ref.shape[0],
        embed_ref.shape[0],
        padded,
        onehot,
        table_hi,
        table_lo,
        pooled,
    )
    wide = feat.astype(F32)
    half_sq = -0.5 * jnp.sum(wide * wide, axis=0, keepdims=True)
    cols_ref[:channels, :] = feat
    high = half_sq.astype(BF16).astype(F32)
    middle = (half_sq - high).astype(BF16).astype(F32)
    low = half_sq - high - middle
    order = lax.broadcasted_iota(jnp.int32, (EXTRA, rows), 0)
    tail = jnp.where(order == 0, high, jnp.where(order == 1, middle, jnp.where(order == 2, low, 0.0)))
    cols_ref[channels:, :] = tail.astype(BF16)
    rows_ref[...] = wide.T.astype(BF16)


def apply_kernel(hyper_ref, rows_ref, cols_ref, probes_ref, own_ref, prev_ref, coupling_ref, x_ref, gram_ref, total):
    rows, channels = rows_ref.shape
    blocks = cols_ref.shape[0]
    all_rows = blocks * rows
    width = prev_ref.shape[1]
    wide = rows_ref[...].astype(F32)
    row_half = -0.5 * jnp.sum(wide * wide, axis=1, keepdims=True)
    amplitude = hyper_ref[0]
    total[...] = jnp.zeros_like(total)

    def block_step(block, carry):
        cols = cols_ref[block, :channels, :]
        tail = cols_ref[block, channels:, :].astype(F32)
        col_half = jnp.sum(tail, axis=0, keepdims=True)
        inner = jnp.dot(rows_ref[...], cols, preferred_element_type=F32)
        exponent = jnp.minimum(inner + (row_half + col_half), 0.0)
        weights = (amplitude * jnp.exp(exponent)).astype(BF16)
        start = pl.multiple_of(block * rows, rows)
        total[...] += jnp.dot(weights, probes_ref[pl.ds(start, rows), :], preferred_element_type=F32)
        return carry

    lax.fori_loop(0, blocks, block_step, 0)
    first = pl.multiple_of(lax.axis_index("rep") * rows, rows)
    own = own_ref[pl.ds(first, rows), :].astype(F32)
    root = 1.0 / math.sqrt(all_rows)
    coupled = lax.dot_general(
        prev_ref[...].astype(F32),
        coupling_ref[...],
        (((1,), (1,)), ((), ())),
        precision=HIGH,
        preferred_element_type=F32,
    )
    x_ref[:, :width] = own * root
    x_ref[:, width:] = (total[...] + hyper_ref[1] * own - coupled) * root
    both = x_ref[...]
    gram_ref[...] = jnp.dot(both.T, both, precision=HIGH, preferred_element_type=F32)


def finish_kernel(root, x_ref, sums_ref, a_ref, r_ref, next_ref):
    width = a_ref.shape[0]
    corr = sums_ref[:width, :width]
    block_a = sums_ref[:width, width:]
    cross = sums_ref[width:, width:]
    a_ref[...] = block_a
    resid = x_ref[:, width:] - jnp.dot(x_ref[:, :width], block_a, precision=HIGH, preferred_element_type=F32)
    middle = jnp.dot(corr, block_a, precision=HIGH, preferred_element_type=F32) - 2.0 * block_a
    gram = cross + jnp.dot(block_a.T, middle, precision=HIGH, preferred_element_type=F32)
    row = lax.broadcasted_iota(jnp.int32, (width, width), 0)
    col = lax.broadcasted_iota(jnp.int32, (width, width), 1)
    eye = jnp.where(row == col, 1.0, 0.0)
    work = jnp.concatenate([gram, eye], axis=1)
    done = []
    for step in range(width):
        line = work[step : step + 1, :]
        scale = lax.rsqrt(work[step : step + 1, step : step + 1])
        line = line * scale
        done.append(line)
        if step + 1 < width:
            work = work - (work[:, step : step + 1] * scale) * line
    factor = jnp.concatenate(done, axis=0)
    r_ref[...] = jnp.where(row <= col, factor[:, :width], 0.0)
    inverse = factor[:, width:].T
    next_ref[...] = jnp.dot(resid, inverse, precision=HIGH, preferred_element_type=F32) * root


VMEM = pl.BlockSpec(memory_space=pltpu.VMEM)
SMEM = pl.BlockSpec(memory_space=pltpu.SMEM)
PARAMS = pltpu.CompilerParams(vmem_limit_bytes=48 * 1024 * 1024)


def per_device(tokens, lengths, embed, conv_w, conv_b, inv_len, hyper, probes, prev_probes, coupling):
    rows, width = prev_probes.shape
    vocab, channels = embed.shape
    taps = conv_w.shape[0]
    seq = tokens.shape[1]
    depth = taps * vocab
    cols, own_rows = pl.pallas_call(
        feature_kernel,
        out_shape=(
            jax.ShapeDtypeStruct((channels + EXTRA, rows), BF16),
            jax.ShapeDtypeStruct((rows, channels), BF16),
        ),
        in_specs=[VMEM] * 6,
        out_specs=(VMEM, VMEM),
        scratch_shapes=[
            pltpu.VMEM((rows, 128), jnp.int32),
            pltpu.VMEM((seq * vocab, rows), BF16),
            pltpu.VMEM((depth, channels), F32),
            pltpu.VMEM((channels, depth), BF16),
            pltpu.VMEM((channels, depth), BF16),
            pltpu.VMEM((channels, rows), F32),
        ],
        compiler_params=PARAMS,
    )(tokens, lengths.reshape(1, -1), embed, conv_w, conv_b.reshape(1, -1), inv_len.reshape(-1, 1))
    all_cols = lax.all_gather(cols, ("blk", "rep"), axis=0)
    all_probes = lax.all_gather(probes, "blk", axis=0, tiled=True)
    pair, gram = pl.pallas_call(
        apply_kernel,
        out_shape=(
            jax.ShapeDtypeStruct((rows, 2 * width), F32),
            jax.ShapeDtypeStruct((2 * width, 2 * width), F32),
        ),
        in_specs=[SMEM] + [VMEM] * 6,
        out_specs=(VMEM, VMEM),
        scratch_shapes=[pltpu.VMEM((rows, width), F32)],
        compiler_params=PARAMS,
    )(hyper, own_rows, all_cols, all_probes, probes, prev_probes, coupling)
    sums = lax.psum(gram, ("blk", "rep"))
    root = math.sqrt(all_probes.shape[0])
    return pl.pallas_call(
        functools.partial(finish_kernel, root),
        out_shape=(
            jax.ShapeDtypeStruct((width, width), F32),
            jax.ShapeDtypeStruct((width, width), F32),
            jax.ShapeDtypeStruct((rows, width), F32),
        ),
        in_specs=[VMEM] * 2,
        out_specs=(VMEM, VMEM, VMEM),
        compiler_params=PARAMS,
    )(pair, sums)


def solution(mesh):
    return jax.shard_map(
        per_device,
        mesh=mesh,
        in_specs=(
            P("blk", None),
            P("blk"),
            P(),
            P(),
            P(),
            P(),
            P(),
            P("blk", None),
            P(("blk", "rep"), None),
            P(),
        ),
        out_specs=(P(), P(), P(("blk", "rep"), None)),
        check_vma=False,
    )
```

```python
import functools
import math

import jax
import jax.numpy as jnp
from jax import lax
from jax.experimental import pallas as pl
from jax.experimental.pallas import tpu as pltpu
from jax.sharding import PartitionSpec as P

F32 = jnp.float32
BF16 = jnp.bfloat16
EXTRA = 16
LINE = 4
HIGH = lax.Precision.HIGHEST


def build_table(embed_ref, conv_w_ref, conv_b_ref, table, table_hi, table_lo):
    taps, width, channels = conv_w_ref.shape
    vocab = embed_ref.shape[0]
    groups = channels // width
    in_group = lax.broadcasted_iota(jnp.int32, (channels, channels), 0) // width
    out_group = lax.broadcasted_iota(jnp.int32, (channels, channels), 1) // width
    same = in_group == out_group
    for tap in range(taps):
        tiled = jnp.concatenate([conv_w_ref[tap].astype(F32)] * groups, axis=0)
        dense = jnp.where(same, tiled, 0.0).astype(BF16)
        entry = jnp.dot(embed_ref[...], dense, preferred_element_type=F32)
        if tap == 0:
            entry = entry + conv_b_ref[...]
        table[tap * vocab : (tap + 1) * vocab, :] = entry
    full = table[...].T
    high = full.astype(BF16)
    table_hi[...] = high
    table_lo[...] = (full - high.astype(F32)).astype(BF16)


def pooled_features(
    tokens_ref, lengths_ref, inv_len_ref, first, rows, taps, vocab, padded, onehot, table_hi, table_lo, pooled
):
    seq = tokens_ref.shape[1]
    channels = inv_len_ref.shape[0]
    positions = (seq - taps) // 2 + 1
    padded[...] = jnp.zeros_like(padded)
    padded[:, :seq] = tokens_ref[pl.ds(first, rows), :]
    token_rows = padded[...].T
    vocab_ids = lax.broadcasted_iota(jnp.int32, (vocab, rows), 0)
    for spot in range(seq):
        hit = jnp.broadcast_to(token_rows[spot : spot + 1, :], (vocab, rows)) == vocab_ids
        onehot[spot * vocab : (spot + 1) * vocab, :] = jnp.where(hit, 1.0, 0.0).astype(BF16)
    counts = (lengths_ref[:, pl.ds(first, rows)] - taps) // 2 + 1
    pooled[...] = jnp.zeros_like(pooled)
    root = math.sqrt(2.0 / math.pi)

    def position_step(position, carry):
        start = pl.multiple_of(position * (2 * vocab), 2 * vocab)
        window = onehot[pl.ds(start, taps * vocab), :]
        preact = jnp.dot(table_hi[...], window, preferred_element_type=F32)
        preact = preact + jnp.dot(table_lo[...], window, preferred_element_type=F32)
        inner = preact * (root + (root * 0.044715) * (preact * preact))
        half = jnp.where(position < counts, 0.5, 0.0)
        weighted = preact * half
        pooled[...] += weighted + weighted * jnp.tanh(inner)
        return carry

    lax.fori_loop(0, positions, position_step, 0)
    mean_pool = pooled[...] / counts.astype(F32)
    centered = mean_pool - jnp.mean(mean_pool, axis=0, keepdims=True)
    variance = jnp.mean(centered * centered, axis=0, keepdims=True)
    normed = centered * lax.rsqrt(variance + 1e-05)
    return (normed * inv_len_ref[...]).astype(BF16)


def feature_kernel(
    tokens_ref,
    lengths_ref,
    embed_ref,
    conv_w_ref,
    conv_b_ref,
    inv_len_ref,
    probes_ref,
    cols_ref,
    rows_ref,
    padded,
    onehot,
    table,
    table_hi,
    table_lo,
    pooled,
):
    rows = cols_ref.shape[1]
    channels = inv_len_ref.shape[0]
    first = pl.multiple_of(lax.axis_index("rep") * rows, rows)
    build_table(embed_ref, conv_w_ref, conv_b_ref, table, table_hi, table_lo)
    feat = pooled_features(
        tokens_ref,
        lengths_ref,
        inv_len_ref,
        first,
        rows,
        conv_w_ref.shape[0],
        embed_ref.shape[0],
        padded,
        onehot,
        table_hi,
        table_lo,
        pooled,
    )
    wide = feat.astype(F32)
    half_sq = -0.5 * jnp.sum(wide * wide, axis=0, keepdims=True)
    cols_ref[:channels, :] = feat
    high = half_sq.astype(BF16).astype(F32)
    middle = (half_sq - high).astype(BF16).astype(F32)
    low = half_sq - high - middle
    order = lax.broadcasted_iota(jnp.int32, (EXTRA, rows), 0)
    tail = jnp.where(order == 0, high, jnp.where(order == 1, middle, jnp.where(order == 2, low, 0.0)))
    cols_ref[channels : channels + EXTRA, :] = tail.astype(BF16)
    cols_ref[channels + EXTRA :, :] = probes_ref[pl.ds(first, rows), :].astype(F32).T.astype(BF16)
    rows_ref[...] = wide.T.astype(BF16)


def apply_kernel(
    hyper_ref,
    rows_ref,
    cols_ref,
    own_ref,
    prev_ref,
    coupling_ref,
    x_ref,
    sums_ref,
    row_blocks,
    col_blocks,
    row_halves,
    totals,
    partial_out,
    partial_in,
    gram_out,
    gram_in,
    line_in,
    gathered,
    row_send,
    row_recv,
    col_send,
    col_recv,
    partial_send,
    partial_recv,
    gram_send,
    gram_recv,
    line_send,
    line_recv,
    gather_send,
    gather_recv,
):
    rows, channels = rows_ref.shape
    plane = row_blocks.shape[0]
    line = col_blocks.shape[0]
    width = prev_ref.shape[1]
    reps = lax.axis_size("rep")
    low = plane // reps
    blk = lax.axis_index("blk")
    rep = lax.axis_index("rep")
    my_line = blk // low
    my_plane = lax.rem(blk, low) * reps + rep

    def plane_id(spot):
        return {"blk": my_line * low + spot // reps, "rep": lax.rem(spot, reps)}

    def line_id(spot):
        return {"blk": spot * low + lax.rem(blk, low), "rep": rep}

    def plane_peer(step):
        return lax.rem(my_plane + step, plane)

    line_peers = [my_line, my_line + 1 - 2 * lax.rem(my_line, 2), lax.rem(my_line + 2, 4), 3 - my_line]

    def copy(src, dst, send_sem, recv_sem, device):
        return pltpu.make_async_remote_copy(
            src_ref=src,
            dst_ref=dst,
            send_sem=send_sem,
            recv_sem=recv_sem,
            device_id=device,
            device_id_type=pl.DeviceIdType.MESH,
        )

    def each_plane_peer(action):
        def body(step, carry):
            action(step, plane_peer(step))
            return carry

        lax.fori_loop(1, plane, body, 0)

    barrier = pltpu.get_barrier_semaphore()

    def greet(step, peer):
        pl.semaphore_signal(barrier, inc=1, device_id=plane_id(peer), device_id_type=pl.DeviceIdType.MESH)

    each_plane_peer(greet)
    for peer in line_peers[1:]:
        pl.semaphore_signal(barrier, inc=1, device_id=line_id(peer), device_id_type=pl.DeviceIdType.MESH)
    pl.semaphore_wait(barrier, plane - 1 + line - 1)

    def col_copy(order, slot, peer):
        return copy(cols_ref, col_blocks.at[slot], col_send.at[order], col_recv.at[slot], line_id(peer))

    def row_copy(step, slot, peer):
        return copy(rows_ref, row_blocks.at[slot], row_send.at[step], row_recv.at[slot], plane_id(peer))

    col_copy(1, my_line, line_peers[1]).start()
    each_plane_peer(lambda step, peer: row_copy(step, my_plane, peer).start())
    col_copy(2, my_line, line_peers[2]).start()
    col_copy(3, my_line, line_peers[3]).start()
    row_blocks[my_plane] = rows_ref[...]
    col_blocks[my_line] = cols_ref[...]
    amplitude = hyper_ref[0]

    def partial_copy(step, slot, peer):
        return copy(
            partial_out.at[step], partial_in.at[slot], partial_send.at[step], partial_recv.at[slot], plane_id(peer)
        )

    def packed(value):
        return jnp.concatenate([value[: rows // 2, :], value[rows // 2 :, :]], axis=1)

    for order in range(line):
        source = line_peers[order]
        if order:
            col_copy(order, source, source).wait_recv()
        cols = col_blocks.at[source]
        col_half = jnp.sum(cols[channels : channels + EXTRA, :].astype(F32), axis=0, keepdims=True)
        block_probes = cols[channels + EXTRA :, :].astype(F32).T.astype(BF16)
        last = order == line - 1

        def pair_step(pair, carry, order=order, cols=cols, col_half=col_half, block_probes=block_probes, last=last):
            for part in range(2):
                step = 2 * pair + part + (1 if last else 0)
                spot = plane_peer(step)
                if order == 0:

                    @pl.when(step > 0)
                    def _():
                        row_copy(step, spot, spot).wait_recv()

                    wide = row_blocks[spot].astype(F32)
                    row_halves[spot] = -0.5 * jnp.sum(wide * wide, axis=1, keepdims=True)
            for part in range(2):
                step = 2 * pair + part + (1 if last else 0)
                spot = plane_peer(step)
                inner = jnp.dot(row_blocks[spot], cols[:channels, :], preferred_element_type=F32)
                exponent = jnp.minimum(inner + (row_halves[spot] + col_half), 0.0)
                weights = (amplitude * jnp.exp(exponent)).astype(BF16)
                value = jnp.dot(weights, block_probes, preferred_element_type=F32)
                if order:
                    value = value + totals[spot]
                if last:
                    partial_out[step] = packed(value)
                else:
                    totals[spot] = value
            if last:
                for part in range(2):
                    step = 2 * pair + part + 1
                    spot = plane_peer(step)

                    @pl.when(step < plane)
                    def _():
                        partial_copy(step, my_plane, spot).start()

            return carry

        lax.fori_loop(0, plane // 2, pair_step, 0)

    own = own_ref[pl.ds(pl.multiple_of(rep * rows, rows), rows), :].astype(F32)
    root = 1.0 / math.sqrt(rows * plane * line)
    coupled = lax.dot_general(
        prev_ref[...].astype(F32),
        coupling_ref[...],
        (((1,), (1,)), ((), ())),
        precision=HIGH,
        preferred_element_type=F32,
    )

    def add_partial(step, total):
        spot = plane_peer(step)
        partial_copy(step, spot, spot).wait_recv()
        return total + partial_in[spot]

    total = lax.fori_loop(1, plane, add_partial, partial_out[plane])
    applied = jnp.concatenate([total[:, :width], total[:, width:]], axis=0)
    x_ref[:, :width] = own * root
    x_ref[:, width:] = (applied + hyper_ref[1] * own - coupled) * root
    both = x_ref[...]
    gram = jnp.dot(both.T, both, precision=HIGH, preferred_element_type=F32)
    piece = gram_out.shape[1]
    for spot in range(plane):
        gram_out[spot] = gram[spot * piece : (spot + 1) * piece, :]

    def gram_copy(step, target, slot):
        return copy(gram_out.at[target], gram_in.at[slot], gram_send.at[step], gram_recv.at[slot], plane_id(target))

    each_plane_peer(lambda step, peer: gram_copy(step, peer, my_plane).start())

    def add_gram(step, total):
        spot = plane_peer(step)
        gram_copy(step, spot, spot).wait_recv()
        return total + gram_in[spot]

    line_in[my_line] = lax.fori_loop(1, plane, add_gram, gram_out[my_plane])

    def line_copy(order, slot, peer):
        return copy(line_in.at[my_line], line_in.at[slot], line_send.at[order], line_recv.at[slot], line_id(peer))

    for order in range(1, line):
        line_copy(order, my_line, line_peers[order]).start()
    for order in range(1, line):
        line_copy(order, line_peers[order], line_peers[order]).wait_recv()
    gathered[my_plane] = (line_in[0] + line_in[1]) + (line_in[2] + line_in[3])

    def gather_copy(step, slot, peer):
        return copy(
            gathered.at[my_plane], gathered.at[slot], gather_send.at[step], gather_recv.at[slot], plane_id(peer)
        )

    each_plane_peer(lambda step, peer: gather_copy(step, my_plane, peer).start())
    each_plane_peer(lambda step, peer: gather_copy(step, peer, peer).wait_recv())
    for spot in range(plane):
        sums_ref[spot * piece : (spot + 1) * piece, :] = gathered[spot]
    for order in range(1, line):
        col_copy(order, my_line, line_peers[order]).wait_send()
        line_copy(order, my_line, line_peers[order]).wait_send()

    def drain(step, peer):
        row_copy(step, my_plane, peer).wait_send()
        partial_copy(step, my_plane, peer).wait_send()
        gram_copy(step, peer, my_plane).wait_send()
        gather_copy(step, my_plane, peer).wait_send()

    each_plane_peer(drain)


def finish_kernel(root, x_ref, sums_ref, a_ref, r_ref, next_ref):
    width = a_ref.shape[0]
    corr = sums_ref[:width, :width]
    block_a = sums_ref[:width, width:]
    cross = sums_ref[width:, width:]
    a_ref[...] = block_a
    resid = x_ref[:, width:] - jnp.dot(x_ref[:, :width], block_a, precision=HIGH, preferred_element_type=F32)
    middle = jnp.dot(corr, block_a, precision=HIGH, preferred_element_type=F32) - 2.0 * block_a
    gram = cross + jnp.dot(block_a.T, middle, precision=HIGH, preferred_element_type=F32)
    row = lax.broadcasted_iota(jnp.int32, (width, width), 0)
    col = lax.broadcasted_iota(jnp.int32, (width, width), 1)
    eye = jnp.where(row == col, 1.0, 0.0)
    work = jnp.concatenate([gram, eye], axis=1)
    done = []
    for step in range(width):
        line = work[step : step + 1, :]
        scale = lax.rsqrt(work[step : step + 1, step : step + 1])
        line = line * scale
        done.append(line)
        if step + 1 < width:
            work = work - (work[:, step : step + 1] * scale) * line
    factor = jnp.concatenate(done, axis=0)
    r_ref[...] = jnp.where(row <= col, factor[:, :width], 0.0)
    inverse = factor[:, width:].T
    next_ref[...] = jnp.dot(resid, inverse, precision=HIGH, preferred_element_type=F32) * root


VMEM = pl.BlockSpec(memory_space=pltpu.VMEM)
SMEM = pl.BlockSpec(memory_space=pltpu.SMEM)
PARAMS = pltpu.CompilerParams(vmem_limit_bytes=48 * 1024 * 1024)


def per_device(tokens, lengths, embed, conv_w, conv_b, inv_len, hyper, probes, prev_probes, coupling):
    rows, width = prev_probes.shape
    vocab, channels = embed.shape
    taps = conv_w.shape[0]
    seq = tokens.shape[1]
    depth = taps * vocab
    cols, own_rows = pl.pallas_call(
        feature_kernel,
        out_shape=(
            jax.ShapeDtypeStruct((channels + EXTRA + width, rows), BF16),
            jax.ShapeDtypeStruct((rows, channels), BF16),
        ),
        in_specs=[VMEM] * 7,
        out_specs=(VMEM, VMEM),
        scratch_shapes=[
            pltpu.VMEM((rows, 128), jnp.int32),
            pltpu.VMEM((seq * vocab, rows), BF16),
            pltpu.VMEM((depth, channels), F32),
            pltpu.VMEM((channels, depth), BF16),
            pltpu.VMEM((channels, depth), BF16),
            pltpu.VMEM((channels, rows), F32),
        ],
        compiler_params=PARAMS,
    )(tokens, lengths.reshape(1, -1), embed, conv_w, conv_b.reshape(1, -1), inv_len.reshape(-1, 1), probes)
    line = LINE
    plane = lax.axis_size("blk") // line * lax.axis_size("rep")
    piece = 2 * width // plane
    dma = pltpu.SemaphoreType.DMA
    pair, sums = pl.pallas_call(
        apply_kernel,
        out_shape=(
            jax.ShapeDtypeStruct((rows, 2 * width), F32),
            jax.ShapeDtypeStruct((2 * width, 2 * width), F32),
        ),
        in_specs=[SMEM] + [VMEM] * 5,
        out_specs=(VMEM, VMEM),
        scratch_shapes=[
            pltpu.VMEM((plane, rows, channels), BF16),
            pltpu.VMEM((line, channels + EXTRA + width, rows), BF16),
            pltpu.VMEM((plane, rows, 1), F32),
            pltpu.VMEM((plane, rows, width), F32),
            pltpu.VMEM((plane + 1, rows // 2, 2 * width), F32),
            pltpu.VMEM((plane, rows // 2, 2 * width), F32),
            pltpu.VMEM((plane, piece, 2 * width), F32),
            pltpu.VMEM((plane, piece, 2 * width), F32),
            pltpu.VMEM((line, piece, 2 * width), F32),
            pltpu.VMEM((plane, piece, 2 * width), F32),
            dma((plane,)),
            dma((plane,)),
            dma((line,)),
            dma((line,)),
            dma((plane,)),
            dma((plane,)),
            dma((plane,)),
            dma((plane,)),
            dma((line,)),
            dma((line,)),
            dma((plane,)),
            dma((plane,)),
        ],
        compiler_params=pltpu.CompilerParams(
            vmem_limit_bytes=48 * 1024 * 1024, collective_id=0, has_side_effects=True
        ),
    )(hyper, own_rows, cols, probes, prev_probes, coupling)
    root = math.sqrt(rows * plane * line)
    return pl.pallas_call(
        functools.partial(finish_kernel, root),
        out_shape=(
            jax.ShapeDtypeStruct((width, width), F32),
            jax.ShapeDtypeStruct((width, width), F32),
            jax.ShapeDtypeStruct((rows, width), F32),
        ),
        in_specs=[VMEM] * 2,
        out_specs=(VMEM, VMEM, VMEM),
        compiler_params=PARAMS,
    )(pair, sums)


def solution(mesh):
    return jax.shard_map(
        per_device,
        mesh=mesh,
        in_specs=(
            P("blk", None),
            P("blk"),
            P(),
            P(),
            P(),
            P(),
            P(),
            P("blk", None),
            P(("blk", "rep"), None),
            P(),
        ),
        out_specs=(P(), P(), P(("blk", "rep"), None)),
        check_vma=False,
    )
```

```python
import functools
import math

import jax
import jax.numpy as jnp
from jax import lax
from jax.experimental import pallas as pl
from jax.experimental.pallas import tpu as pltpu
from jax.sharding import PartitionSpec as P

F32 = jnp.float32
BF16 = jnp.bfloat16
EXTRA = 16
LINE = 4
HIGH = lax.Precision.HIGHEST


def build_table(embed_ref, conv_w_ref, conv_b_ref, table, table_hi, table_lo):
    taps, width, channels = conv_w_ref.shape
    vocab = embed_ref.shape[0]
    groups = channels // width
    in_group = lax.broadcasted_iota(jnp.int32, (channels, channels), 0) // width
    out_group = lax.broadcasted_iota(jnp.int32, (channels, channels), 1) // width
    same = in_group == out_group
    for tap in range(taps):
        tiled = jnp.concatenate([conv_w_ref[tap].astype(F32)] * groups, axis=0)
        dense = jnp.where(same, tiled, 0.0).astype(BF16)
        entry = jnp.dot(embed_ref[...], dense, preferred_element_type=F32)
        if tap == 0:
            entry = entry + conv_b_ref[...]
        table[tap * vocab : (tap + 1) * vocab, :] = entry
    full = table[...].T
    high = full.astype(BF16)
    table_hi[...] = high
    table_lo[...] = (full - high.astype(F32)).astype(BF16)


def pooled_features(
    tokens_ref, lengths_ref, inv_len_ref, first, rows, taps, vocab, padded, onehot, table_hi, table_lo, pooled
):
    seq = tokens_ref.shape[1]
    channels = inv_len_ref.shape[0]
    positions = (seq - taps) // 2 + 1
    padded[...] = jnp.zeros_like(padded)
    padded[:, :seq] = tokens_ref[pl.ds(first, rows), :]
    token_rows = padded[...].T
    vocab_ids = lax.broadcasted_iota(jnp.int32, (vocab, rows), 0)
    for spot in range(seq):
        hit = jnp.broadcast_to(token_rows[spot : spot + 1, :], (vocab, rows)) == vocab_ids
        onehot[spot * vocab : (spot + 1) * vocab, :] = jnp.where(hit, 1.0, 0.0).astype(BF16)
    counts = (lengths_ref[:, pl.ds(first, rows)] - taps) // 2 + 1
    pooled[...] = jnp.zeros_like(pooled)
    root = math.sqrt(2.0 / math.pi)

    def position_step(position, carry):
        start = pl.multiple_of(position * (2 * vocab), 2 * vocab)
        window = onehot[pl.ds(start, taps * vocab), :]
        preact = jnp.dot(table_hi[...], window, preferred_element_type=F32)
        preact = preact + jnp.dot(table_lo[...], window, preferred_element_type=F32)
        inner = preact * (root + (root * 0.044715) * (preact * preact))
        half = jnp.where(position < counts, 0.5, 0.0)
        weighted = preact * half
        pooled[...] += weighted + weighted * jnp.tanh(inner)
        return carry

    lax.fori_loop(0, positions, position_step, 0)
    mean_pool = pooled[...] / counts.astype(F32)
    centered = mean_pool - jnp.mean(mean_pool, axis=0, keepdims=True)
    variance = jnp.mean(centered * centered, axis=0, keepdims=True)
    normed = centered * lax.rsqrt(variance + 1e-05)
    return (normed * inv_len_ref[...]).astype(BF16)


def feature_kernel(
    tokens_ref,
    lengths_ref,
    embed_ref,
    conv_w_ref,
    conv_b_ref,
    inv_len_ref,
    probes_ref,
    cols_ref,
    rows_ref,
    padded,
    onehot,
    table,
    table_hi,
    table_lo,
    pooled,
):
    rows = cols_ref.shape[1]
    channels = inv_len_ref.shape[0]
    first = pl.multiple_of(lax.axis_index("rep") * rows, rows)
    build_table(embed_ref, conv_w_ref, conv_b_ref, table, table_hi, table_lo)
    feat = pooled_features(
        tokens_ref,
        lengths_ref,
        inv_len_ref,
        first,
        rows,
        conv_w_ref.shape[0],
        embed_ref.shape[0],
        padded,
        onehot,
        table_hi,
        table_lo,
        pooled,
    )
    wide = feat.astype(F32)
    half_sq = -0.5 * jnp.sum(wide * wide, axis=0, keepdims=True)
    cols_ref[:channels, :] = feat
    high = half_sq.astype(BF16).astype(F32)
    middle = (half_sq - high).astype(BF16).astype(F32)
    low = half_sq - high - middle
    order = lax.broadcasted_iota(jnp.int32, (EXTRA, rows), 0)
    tail = jnp.where(order == 0, high, jnp.where(order == 1, middle, jnp.where(order == 2, low, 0.0)))
    cols_ref[channels : channels + EXTRA, :] = tail.astype(BF16)
    cols_ref[channels + EXTRA :, :] = probes_ref[pl.ds(first, rows), :].astype(F32).T.astype(BF16)
    rows_ref[...] = wide.T.astype(BF16)


def apply_kernel(
    hyper_ref,
    rows_ref,
    cols_ref,
    own_ref,
    prev_ref,
    coupling_ref,
    x_ref,
    sums_ref,
    row_blocks,
    col_blocks,
    row_halves,
    totals,
    partial_out,
    partial_in,
    gram_out,
    gram_in,
    line_in,
    gathered,
    row_send,
    row_recv,
    up_send,
    down_send,
    col_recv,
    side_send,
    side_recv,
    partial_send,
    partial_recv,
    gram_send,
    gram_recv,
    line_send,
    line_recv,
    gather_send,
    gather_recv,
):
    rows, channels = rows_ref.shape
    mates = row_blocks.shape[0]
    line = col_blocks.shape[0]
    plane = gram_out.shape[0]
    width = prev_ref.shape[1]
    reps = lax.axis_size("rep")
    low = plane // reps
    blk = lax.axis_index("blk")
    rep = lax.axis_index("rep")
    core = lax.rem(blk, 2)
    other = 1 - core
    mine = blk // low
    my_plane = lax.rem(blk, low) * reps + rep
    my_mate = (lax.rem(blk, low) // 2) * reps + rep

    def plane_id(spot):
        return {"blk": mine * low + spot // reps, "rep": lax.rem(spot, reps)}

    def mate_id(spot):
        return {"blk": mine * low + (spot // reps) * 2 + core, "rep": lax.rem(spot, reps)}

    def line_id(spot):
        return {"blk": spot * low + lax.rem(blk, low), "rep": rep}

    sibling = {"blk": blk + 1 - 2 * core, "rep": rep}

    def plane_peer(step):
        return lax.rem(my_plane + step, plane)

    def mate_peer(step):
        return lax.rem(my_mate + step, mates)

    line_peers = [mine, mine + 1 - 2 * lax.rem(mine, 2), lax.rem(mine + 2, 4), 3 - mine]

    def copy(src, dst, send_sem, recv_sem, device):
        return pltpu.make_async_remote_copy(
            src_ref=src,
            dst_ref=dst,
            send_sem=send_sem,
            recv_sem=recv_sem,
            device_id=device,
            device_id_type=pl.DeviceIdType.MESH,
        )

    def each_plane_peer(action):
        def body(step, carry):
            action(step, plane_peer(step))
            return carry

        lax.fori_loop(1, plane, body, 0)

    def each_mate(action):
        def body(step, carry):
            action(step, mate_peer(step))
            return carry

        lax.fori_loop(1, mates, body, 0)

    barrier = pltpu.get_barrier_semaphore()

    def greet(step, peer):
        pl.semaphore_signal(barrier, inc=1, device_id=plane_id(peer), device_id_type=pl.DeviceIdType.MESH)

    each_plane_peer(greet)
    for peer in line_peers[1:]:
        pl.semaphore_signal(barrier, inc=1, device_id=line_id(peer), device_id_type=pl.DeviceIdType.MESH)
    pl.semaphore_wait(barrier, plane - 1 + line - 1)

    def up_copy(slot, src=None):
        src = col_blocks.at[slot, core] if src is None else src
        return copy(src, col_blocks.at[slot, core], up_send.at[slot], col_recv.at[slot], line_id(mine + 1))

    def down_copy(slot, src=None):
        src = col_blocks.at[slot, core] if src is None else src
        return copy(src, col_blocks.at[slot, core], down_send.at[slot], col_recv.at[slot], line_id(mine - 1))

    def side_copy(slot, lane, src=None):
        src = col_blocks.at[slot, lane] if src is None else src
        return copy(src, col_blocks.at[slot, lane], side_send.at[slot], side_recv.at[slot], sibling)

    def row_copy(step, slot, peer):
        return copy(rows_ref, row_blocks.at[slot], row_send.at[step], row_recv.at[slot], mate_id(peer))

    @pl.when(mine < line - 1)
    def _():
        up_copy(mine, cols_ref).start()

    @pl.when(mine > 0)
    def _():
        down_copy(mine, cols_ref).start()

    each_mate(lambda step, peer: row_copy(step, my_mate, peer).start())
    side_copy(mine, core, cols_ref).start()
    row_blocks[my_mate] = rows_ref[...]
    col_blocks[mine, core] = cols_ref[...]
    amplitude = hyper_ref[0]

    def pass_on(distance):
        @pl.when(mine >= distance)
        def _():
            slot = mine - distance
            up_copy(slot).wait_recv()

            @pl.when(mine < line - 1)
            def _():
                up_copy(slot).start()

            side_copy(slot, core).start()

        @pl.when(mine + distance < line)
        def _():
            slot = mine + distance
            down_copy(slot).wait_recv()

            @pl.when(mine > 0)
            def _():
                down_copy(slot).start()

            side_copy(slot, core).start()

    def partial_copy(step, slot, peer):
        return copy(
            partial_out.at[step], partial_in.at[slot], partial_send.at[step], partial_recv.at[slot], mate_id(peer)
        )

    def packed(value):
        return jnp.concatenate([value[: rows // 2, :], value[rows // 2 :, :]], axis=1)

    def column_pass(source, order):
        side_copy(source, other).wait_recv()
        parts = []
        for lane in range(2):
            cols = col_blocks.at[source, lane]
            col_half = jnp.sum(cols[channels : channels + EXTRA, :].astype(F32), axis=0, keepdims=True)
            block_probes = cols[channels + EXTRA :, :].astype(F32).T.astype(BF16)
            parts.append((cols, col_half, block_probes))
        last = order == line - 1

        def pair_step(pair, carry):
            steps = [2 * pair + part + (1 if last else 0) for part in range(2)]
            if order == 0:
                for step in steps:
                    spot = mate_peer(step)

                    @pl.when(step > 0)
                    def _():
                        row_copy(step, spot, spot).wait_recv()

                    wide = row_blocks[spot].astype(F32)
                    row_halves[spot] = -0.5 * jnp.sum(wide * wide, axis=1, keepdims=True)
            for step in steps:
                spot = mate_peer(step)
                value = None if order == 0 else totals[spot]
                for cols, col_half, block_probes in parts:
                    inner = jnp.dot(row_blocks[spot], cols[:channels, :], preferred_element_type=F32)
                    exponent = jnp.minimum(inner + (row_halves[spot] + col_half), 0.0)
                    weights = (amplitude * jnp.exp(exponent)).astype(BF16)
                    term = jnp.dot(weights, block_probes, preferred_element_type=F32)
                    value = term if value is None else value + term
                if last:
                    partial_out[step] = packed(value)
                else:
                    totals[spot] = value
            if last:
                for step in steps:
                    spot = mate_peer(step)

                    @pl.when(step < mates)
                    def _():
                        partial_copy(step, my_mate, spot).start()

            return carry

        lax.fori_loop(0, mates // 2, pair_step, 0)

    second = jnp.where(mine == 0, 1, mine - 1)
    third = jnp.where(mine < 2, 2, jnp.where(mine == 2, 3, 1))
    fourth = jnp.where(mine < 2, 3, 0)
    column_pass(mine, 0)
    pass_on(1)
    column_pass(second, 1)
    pass_on(2)
    column_pass(third, 2)
    pass_on(3)
    column_pass(fourth, 3)

    own = own_ref[pl.ds(pl.multiple_of(rep * rows, rows), rows), :].astype(F32)
    root = 1.0 / math.sqrt(rows * plane * line)
    coupled = lax.dot_general(
        prev_ref[...].astype(F32),
        coupling_ref[...],
        (((1,), (1,)), ((), ())),
        precision=HIGH,
        preferred_element_type=F32,
    )

    def add_partial(step, total):
        spot = mate_peer(step)
        partial_copy(step, spot, spot).wait_recv()
        return total + partial_in[spot]

    total = lax.fori_loop(1, mates, add_partial, partial_out[mates])
    applied = jnp.concatenate([total[:, :width], total[:, width:]], axis=0)
    x_ref[:, :width] = own * root
    x_ref[:, width:] = (applied + hyper_ref[1] * own - coupled) * root
    both = x_ref[...]
    gram = jnp.dot(both.T, both, precision=HIGH, preferred_element_type=F32)
    piece = gram_out.shape[1]
    for spot in range(plane):
        gram_out[spot] = gram[spot * piece : (spot + 1) * piece, :]

    def gram_copy(step, target, slot):
        return copy(gram_out.at[target], gram_in.at[slot], gram_send.at[step], gram_recv.at[slot], plane_id(target))

    each_plane_peer(lambda step, peer: gram_copy(step, peer, my_plane).start())

    def add_gram(step, total):
        spot = plane_peer(step)
        gram_copy(step, spot, spot).wait_recv()
        return total + gram_in[spot]

    line_in[mine] = lax.fori_loop(1, plane, add_gram, gram_out[my_plane])

    def line_copy(order, slot, peer):
        return copy(line_in.at[mine], line_in.at[slot], line_send.at[order], line_recv.at[slot], line_id(peer))

    for order in range(1, line):
        line_copy(order, mine, line_peers[order]).start()
    for order in range(1, line):
        line_copy(order, line_peers[order], line_peers[order]).wait_recv()
    gathered[my_plane] = (line_in[0] + line_in[1]) + (line_in[2] + line_in[3])

    def gather_copy(step, slot, peer):
        return copy(
            gathered.at[my_plane], gathered.at[slot], gather_send.at[step], gather_recv.at[slot], plane_id(peer)
        )

    each_plane_peer(lambda step, peer: gather_copy(step, my_plane, peer).start())
    each_plane_peer(lambda step, peer: gather_copy(step, peer, peer).wait_recv())
    for spot in range(plane):
        sums_ref[spot * piece : (spot + 1) * piece, :] = gathered[spot]
    for order in range(1, line):
        line_copy(order, mine, line_peers[order]).wait_send()
    for slot in range(line):
        side_copy(slot, core).wait_send()

        @pl.when((mine >= slot) & (mine < line - 1))
        def _(slot=slot):
            up_copy(slot).wait_send()

        @pl.when((mine <= slot) & (mine > 0))
        def _(slot=slot):
            down_copy(slot).wait_send()

    def drain_mate(step, peer):
        row_copy(step, my_mate, peer).wait_send()
        partial_copy(step, my_mate, peer).wait_send()

    def drain(step, peer):
        gram_copy(step, peer, my_plane).wait_send()
        gather_copy(step, my_plane, peer).wait_send()

    each_mate(drain_mate)
    each_plane_peer(drain)


def finish_kernel(root, x_ref, sums_ref, a_ref, r_ref, next_ref):
    width = a_ref.shape[0]
    corr = sums_ref[:width, :width]
    block_a = sums_ref[:width, width:]
    cross = sums_ref[width:, width:]
    a_ref[...] = block_a
    resid = x_ref[:, width:] - jnp.dot(x_ref[:, :width], block_a, precision=HIGH, preferred_element_type=F32)
    middle = jnp.dot(corr, block_a, precision=HIGH, preferred_element_type=F32) - 2.0 * block_a
    gram = cross + jnp.dot(block_a.T, middle, precision=HIGH, preferred_element_type=F32)
    row = lax.broadcasted_iota(jnp.int32, (width, width), 0)
    col = lax.broadcasted_iota(jnp.int32, (width, width), 1)
    eye = jnp.where(row == col, 1.0, 0.0)
    work = jnp.concatenate([gram, eye], axis=1)
    done = []
    for step in range(width):
        line = work[step : step + 1, :]
        scale = lax.rsqrt(work[step : step + 1, step : step + 1])
        line = line * scale
        done.append(line)
        if step + 1 < width:
            work = work - (work[:, step : step + 1] * scale) * line
    factor = jnp.concatenate(done, axis=0)
    r_ref[...] = jnp.where(row <= col, factor[:, :width], 0.0)
    inverse = factor[:, width:].T
    next_ref[...] = jnp.dot(resid, inverse, precision=HIGH, preferred_element_type=F32) * root


VMEM = pl.BlockSpec(memory_space=pltpu.VMEM)
SMEM = pl.BlockSpec(memory_space=pltpu.SMEM)
PARAMS = pltpu.CompilerParams(vmem_limit_bytes=48 * 1024 * 1024)


def per_device(tokens, lengths, embed, conv_w, conv_b, inv_len, hyper, probes, prev_probes, coupling):
    rows, width = prev_probes.shape
    vocab, channels = embed.shape
    taps = conv_w.shape[0]
    seq = tokens.shape[1]
    depth = taps * vocab
    cols, own_rows = pl.pallas_call(
        feature_kernel,
        out_shape=(
            jax.ShapeDtypeStruct((channels + EXTRA + width, rows), BF16),
            jax.ShapeDtypeStruct((rows, channels), BF16),
        ),
        in_specs=[VMEM] * 7,
        out_specs=(VMEM, VMEM),
        scratch_shapes=[
            pltpu.VMEM((rows, 128), jnp.int32),
            pltpu.VMEM((seq * vocab, rows), BF16),
            pltpu.VMEM((depth, channels), F32),
            pltpu.VMEM((channels, depth), BF16),
            pltpu.VMEM((channels, depth), BF16),
            pltpu.VMEM((channels, rows), F32),
        ],
        compiler_params=PARAMS,
    )(tokens, lengths.reshape(1, -1), embed, conv_w, conv_b.reshape(1, -1), inv_len.reshape(-1, 1), probes)
    line = LINE
    plane = lax.axis_size("blk") // line * lax.axis_size("rep")
    mates = plane // 2
    piece = 2 * width // plane
    dma = pltpu.SemaphoreType.DMA
    pair, sums = pl.pallas_call(
        apply_kernel,
        out_shape=(
            jax.ShapeDtypeStruct((rows, 2 * width), F32),
            jax.ShapeDtypeStruct((2 * width, 2 * width), F32),
        ),
        in_specs=[SMEM] + [VMEM] * 5,
        out_specs=(VMEM, VMEM),
        scratch_shapes=[
            pltpu.VMEM((mates, rows, channels), BF16),
            pltpu.VMEM((line, 2, channels + EXTRA + width, rows), BF16),
            pltpu.VMEM((mates, rows, 1), F32),
            pltpu.VMEM((mates, rows, width), F32),
            pltpu.VMEM((mates + 1, rows // 2, 2 * width), F32),
            pltpu.VMEM((mates, rows // 2, 2 * width), F32),
            pltpu.VMEM((plane, piece, 2 * width), F32),
            pltpu.VMEM((plane, piece, 2 * width), F32),
            pltpu.VMEM((line, piece, 2 * width), F32),
            pltpu.VMEM((plane, piece, 2 * width), F32),
            dma((mates,)),
            dma((mates,)),
            dma((line,)),
            dma((line,)),
            dma((line,)),
            dma((line,)),
            dma((line,)),
            dma((mates,)),
            dma((mates,)),
            dma((plane,)),
            dma((plane,)),
            dma((line,)),
            dma((line,)),
            dma((plane,)),
            dma((plane,)),
        ],
        compiler_params=pltpu.CompilerParams(
            vmem_limit_bytes=48 * 1024 * 1024, collective_id=0, has_side_effects=True
        ),
    )(hyper, own_rows, cols, probes, prev_probes, coupling)
    root = math.sqrt(rows * plane * line)
    return pl.pallas_call(
        functools.partial(finish_kernel, root),
        out_shape=(
            jax.ShapeDtypeStruct((width, width), F32),
            jax.ShapeDtypeStruct((width, width), F32),
            jax.ShapeDtypeStruct((rows, width), F32),
        ),
        in_specs=[VMEM] * 2,
        out_specs=(VMEM, VMEM, VMEM),
        compiler_params=PARAMS,
    )(pair, sums)


def solution(mesh):
    return jax.shard_map(
        per_device,
        mesh=mesh,
        in_specs=(
            P("blk", None),
            P("blk"),
            P(),
            P(),
            P(),
            P(),
            P(),
            P("blk", None),
            P(("blk", "rep"), None),
            P(),
        ),
        out_specs=(P(), P(), P(("blk", "rep"), None)),
        check_vma=False,
    )
```

```python
import functools
import math

import jax
import jax.numpy as jnp
from jax import lax
from jax.experimental import pallas as pl
from jax.experimental.pallas import tpu as pltpu
from jax.sharding import PartitionSpec as P

F32 = jnp.float32
BF16 = jnp.bfloat16
EXTRA = 16
LINE = 4
GROUP = 4
PANEL = 4
HIGH = lax.Precision.HIGHEST


def build_table(embed_ref, conv_w_ref, conv_b_ref, table, table_hi, table_lo):
    taps, width, channels = conv_w_ref.shape
    vocab = embed_ref.shape[0]
    groups = channels // width
    in_group = lax.broadcasted_iota(jnp.int32, (channels, channels), 0) // width
    out_group = lax.broadcasted_iota(jnp.int32, (channels, channels), 1) // width
    same = in_group == out_group
    for tap in range(taps):
        tiled = jnp.concatenate([conv_w_ref[tap].astype(F32)] * groups, axis=0)
        dense = jnp.where(same, tiled, 0.0).astype(BF16)
        entry = jnp.dot(embed_ref[...], dense, preferred_element_type=F32)
        if tap == 0:
            entry = entry + conv_b_ref[...]
        table[tap * vocab : (tap + 1) * vocab, :] = entry
    full = table[...].T
    high = full.astype(BF16)
    table_hi[...] = high
    table_lo[...] = (full - high.astype(F32)).astype(BF16)


def pooled_features(
    tokens_ref, lengths_ref, inv_len_ref, first, rows, taps, vocab, padded, onehot, table_hi, table_lo, pooled
):
    seq = tokens_ref.shape[1]
    channels = inv_len_ref.shape[0]
    positions = (seq - taps) // 2 + 1
    padded[...] = jnp.zeros_like(padded)
    padded[:, :seq] = tokens_ref[pl.ds(first, rows), :]
    token_rows = padded[...].T
    vocab_ids = lax.broadcasted_iota(jnp.int32, (vocab, rows), 0)
    for spot in range(seq):
        hit = jnp.broadcast_to(token_rows[spot : spot + 1, :], (vocab, rows)) == vocab_ids
        onehot[spot * vocab : (spot + 1) * vocab, :] = jnp.where(hit, 1.0, 0.0).astype(BF16)
    counts = (lengths_ref[:, pl.ds(first, rows)] - taps) // 2 + 1
    pooled[...] = jnp.zeros_like(pooled)
    root = math.sqrt(2.0 / math.pi)

    def position_step(group, carry):
        total = None
        for part in range(GROUP):
            position = group * GROUP + part
            start = pl.multiple_of(position * (2 * vocab), 2 * vocab)
            window = onehot[pl.ds(start, taps * vocab), :]
            preact = jnp.dot(table_hi[...], window, preferred_element_type=F32)
            preact = preact + jnp.dot(table_lo[...], window, preferred_element_type=F32)
            inner = preact * (root + (root * 0.044715) * (preact * preact))
            half = jnp.where(position < counts, 0.5, 0.0)
            weighted = preact * half
            term = weighted + weighted * jnp.tanh(inner)
            total = term if total is None else total + term
        pooled[...] += total
        return carry

    lax.fori_loop(0, positions // GROUP, position_step, 0)
    mean_pool = pooled[...] / counts.astype(F32)
    centered = mean_pool - jnp.mean(mean_pool, axis=0, keepdims=True)
    variance = jnp.mean(centered * centered, axis=0, keepdims=True)
    normed = centered * lax.rsqrt(variance + 1e-05)
    return (normed * inv_len_ref[...]).astype(BF16)


def feature_kernel(
    tokens_ref,
    lengths_ref,
    embed_ref,
    conv_w_ref,
    conv_b_ref,
    inv_len_ref,
    probes_ref,
    cols_ref,
    rows_ref,
    padded,
    onehot,
    table,
    table_hi,
    table_lo,
    pooled,
):
    rows = cols_ref.shape[1]
    channels = inv_len_ref.shape[0]
    first = pl.multiple_of(lax.axis_index("rep") * rows, rows)
    build_table(embed_ref, conv_w_ref, conv_b_ref, table, table_hi, table_lo)
    feat = pooled_features(
        tokens_ref,
        lengths_ref,
        inv_len_ref,
        first,
        rows,
        conv_w_ref.shape[0],
        embed_ref.shape[0],
        padded,
        onehot,
        table_hi,
        table_lo,
        pooled,
    )
    wide = feat.astype(F32)
    half_sq = -0.5 * jnp.sum(wide * wide, axis=0, keepdims=True)
    cols_ref[:channels, :] = feat
    high = half_sq.astype(BF16).astype(F32)
    middle = (half_sq - high).astype(BF16).astype(F32)
    low = half_sq - high - middle
    order = lax.broadcasted_iota(jnp.int32, (EXTRA, rows), 0)
    tail = jnp.where(order == 0, high, jnp.where(order == 1, middle, jnp.where(order == 2, low, 0.0)))
    cols_ref[channels : channels + EXTRA, :] = tail.astype(BF16)
    cols_ref[channels + EXTRA :, :] = probes_ref[pl.ds(first, rows), :].astype(F32).T.astype(BF16)
    rows_ref[...] = wide.T.astype(BF16)


def apply_kernel(
    hyper_ref,
    rows_ref,
    cols_ref,
    own_ref,
    prev_ref,
    coupling_ref,
    x_ref,
    sums_ref,
    row_blocks,
    col_blocks,
    row_halves,
    totals,
    partial_out,
    partial_in,
    gram_out,
    gram_in,
    line_in,
    gathered,
    row_send,
    row_recv,
    up_send,
    down_send,
    col_recv,
    side_send,
    side_recv,
    partial_send,
    partial_recv,
    gram_send,
    gram_recv,
    line_send,
    line_recv,
    gather_send,
    gather_recv,
):
    rows, channels = rows_ref.shape
    mates = row_blocks.shape[0]
    line = col_blocks.shape[0]
    plane = gram_out.shape[0]
    width = prev_ref.shape[1]
    reps = lax.axis_size("rep")
    low = plane // reps
    blk = lax.axis_index("blk")
    rep = lax.axis_index("rep")
    core = lax.rem(blk, 2)
    other = 1 - core
    mine = blk // low
    my_plane = lax.rem(blk, low) * reps + rep
    my_mate = (lax.rem(blk, low) // 2) * reps + rep

    def plane_id(spot):
        return {"blk": mine * low + spot // reps, "rep": lax.rem(spot, reps)}

    def mate_id(spot):
        return {"blk": mine * low + (spot // reps) * 2 + core, "rep": lax.rem(spot, reps)}

    def line_id(spot):
        return {"blk": spot * low + lax.rem(blk, low), "rep": rep}

    sibling = {"blk": blk + 1 - 2 * core, "rep": rep}

    def plane_peer(step):
        return lax.rem(my_plane + step, plane)

    def mate_peer(step):
        return lax.rem(my_mate + step, mates)

    line_peers = [mine, mine + 1 - 2 * lax.rem(mine, 2), lax.rem(mine + 2, 4), 3 - mine]

    def copy(src, dst, send_sem, recv_sem, device):
        return pltpu.make_async_remote_copy(
            src_ref=src,
            dst_ref=dst,
            send_sem=send_sem,
            recv_sem=recv_sem,
            device_id=device,
            device_id_type=pl.DeviceIdType.MESH,
        )

    def each_plane_peer(action):
        def body(step, carry):
            action(step, plane_peer(step))
            return carry

        lax.fori_loop(1, plane, body, 0)

    def each_mate(action):
        def body(step, carry):
            action(step, mate_peer(step))
            return carry

        lax.fori_loop(1, mates, body, 0)

    barrier = pltpu.get_barrier_semaphore()

    def greet(step, peer):
        pl.semaphore_signal(barrier, inc=1, device_id=plane_id(peer), device_id_type=pl.DeviceIdType.MESH)

    each_plane_peer(greet)
    for peer in line_peers[1:]:
        pl.semaphore_signal(barrier, inc=1, device_id=line_id(peer), device_id_type=pl.DeviceIdType.MESH)
    pl.semaphore_wait(barrier, plane - 1 + line - 1)

    def up_copy(slot, src=None):
        src = col_blocks.at[slot, core] if src is None else src
        return copy(src, col_blocks.at[slot, core], up_send.at[slot], col_recv.at[slot], line_id(mine + 1))

    def down_copy(slot, src=None):
        src = col_blocks.at[slot, core] if src is None else src
        return copy(src, col_blocks.at[slot, core], down_send.at[slot], col_recv.at[slot], line_id(mine - 1))

    def side_copy(slot, lane, src=None):
        src = col_blocks.at[slot, lane] if src is None else src
        return copy(src, col_blocks.at[slot, lane], side_send.at[slot], side_recv.at[slot], sibling)

    def row_copy(step, slot, peer):
        return copy(rows_ref, row_blocks.at[slot], row_send.at[step], row_recv.at[slot], mate_id(peer))

    @pl.when(mine < line - 1)
    def _():
        up_copy(mine, cols_ref).start()

    @pl.when(mine > 0)
    def _():
        down_copy(mine, cols_ref).start()

    each_mate(lambda step, peer: row_copy(step, my_mate, peer).start())
    side_copy(mine, core, cols_ref).start()
    row_blocks[my_mate] = rows_ref[...]
    col_blocks[mine, core] = cols_ref[...]
    amplitude = hyper_ref[0]

    def pass_on(distance):
        @pl.when(mine >= distance)
        def _():
            slot = mine - distance
            up_copy(slot).wait_recv()

            @pl.when(mine < line - 1)
            def _():
                up_copy(slot).start()

            side_copy(slot, core).start()

        @pl.when(mine + distance < line)
        def _():
            slot = mine + distance
            down_copy(slot).wait_recv()

            @pl.when(mine > 0)
            def _():
                down_copy(slot).start()

            side_copy(slot, core).start()

    def partial_copy(step, slot, peer):
        return copy(
            partial_out.at[step], partial_in.at[slot], partial_send.at[step], partial_recv.at[slot], mate_id(peer)
        )

    def packed(value):
        return jnp.concatenate([value[: rows // 2, :], value[rows // 2 :, :]], axis=1)

    def column_pass(source, order):
        side_copy(source, other).wait_recv()
        parts = []
        for lane in range(2):
            cols = col_blocks.at[source, lane]
            col_half = jnp.sum(cols[channels : channels + EXTRA, :].astype(F32), axis=0, keepdims=True)
            block_probes = cols[channels + EXTRA :, :].astype(F32).T.astype(BF16)
            parts.append((cols, col_half, block_probes))
        last = order == line - 1

        group = 1 if order == 0 else 2

        def pair_step(pair, carry):
            steps = [group * pair + part + (1 if last else 0) for part in range(group)]
            if order == 0:
                for step in steps:
                    spot = mate_peer(step)

                    @pl.when(step > 0)
                    def _():
                        row_copy(step, spot, spot).wait_recv()

                    wide = row_blocks[spot].astype(F32)
                    row_halves[spot] = -0.5 * jnp.sum(wide * wide, axis=1, keepdims=True)
            for step in steps:
                spot = mate_peer(step)
                value = None if order == 0 else totals[spot]
                for cols, col_half, block_probes in parts:
                    inner = jnp.dot(row_blocks[spot], cols[:channels, :], preferred_element_type=F32)
                    exponent = jnp.minimum(inner + (row_halves[spot] + col_half), 0.0)
                    weights = (amplitude * jnp.exp(exponent)).astype(BF16)
                    term = jnp.dot(weights, block_probes, preferred_element_type=F32)
                    value = term if value is None else value + term
                if last:
                    partial_out[step] = packed(value)
                else:
                    totals[spot] = value
            if last:
                for step in steps:
                    spot = mate_peer(step)

                    @pl.when(step < mates)
                    def _():
                        partial_copy(step, my_mate, spot).start()

            return carry

        lax.fori_loop(0, mates // group, pair_step, 0)

    second = jnp.where(mine == 0, 1, mine - 1)
    third = jnp.where(mine < 2, 2, jnp.where(mine == 2, 3, 1))
    fourth = jnp.where(mine < 2, 3, 0)
    column_pass(mine, 0)
    pass_on(1)
    column_pass(second, 1)
    pass_on(2)
    column_pass(third, 2)
    pass_on(3)
    column_pass(fourth, 3)

    own = own_ref[pl.ds(pl.multiple_of(rep * rows, rows), rows), :].astype(F32)
    root = 1.0 / math.sqrt(rows * plane * line)
    coupled = lax.dot_general(
        prev_ref[...].astype(F32),
        coupling_ref[...],
        (((1,), (1,)), ((), ())),
        precision=HIGH,
        preferred_element_type=F32,
    )

    def add_partial(step, total):
        spot = mate_peer(step)
        partial_copy(step, spot, spot).wait_recv()
        return total + partial_in[spot]

    total = lax.fori_loop(1, mates, add_partial, partial_out[mates])
    applied = jnp.concatenate([total[:, :width], total[:, width:]], axis=0)
    x_ref[:, :width] = own * root
    x_ref[:, width:] = (applied + hyper_ref[1] * own - coupled) * root
    both = x_ref[...]
    gram = jnp.dot(both.T, both, precision=HIGH, preferred_element_type=F32)
    piece = gram_out.shape[1]
    for spot in range(plane):
        gram_out[spot] = gram[spot * piece : (spot + 1) * piece, :]

    def gram_copy(step, target, slot):
        return copy(gram_out.at[target], gram_in.at[slot], gram_send.at[step], gram_recv.at[slot], plane_id(target))

    each_plane_peer(lambda step, peer: gram_copy(step, peer, my_plane).start())

    def add_gram(step, total):
        spot = plane_peer(step)
        gram_copy(step, spot, spot).wait_recv()
        return total + gram_in[spot]

    line_in[mine] = lax.fori_loop(1, plane, add_gram, gram_out[my_plane])

    def line_copy(order, slot, peer):
        return copy(line_in.at[mine], line_in.at[slot], line_send.at[order], line_recv.at[slot], line_id(peer))

    for order in range(1, line):
        line_copy(order, mine, line_peers[order]).start()
    for order in range(1, line):
        line_copy(order, line_peers[order], line_peers[order]).wait_recv()
    gathered[my_plane] = (line_in[0] + line_in[1]) + (line_in[2] + line_in[3])

    def gather_copy(step, slot, peer):
        return copy(
            gathered.at[my_plane], gathered.at[slot], gather_send.at[step], gather_recv.at[slot], plane_id(peer)
        )

    each_plane_peer(lambda step, peer: gather_copy(step, my_plane, peer).start())
    each_plane_peer(lambda step, peer: gather_copy(step, peer, peer).wait_recv())
    for spot in range(plane):
        sums_ref[spot * piece : (spot + 1) * piece, :] = gathered[spot]
    for order in range(1, line):
        line_copy(order, mine, line_peers[order]).wait_send()
    for slot in range(line):
        side_copy(slot, core).wait_send()

        @pl.when((mine >= slot) & (mine < line - 1))
        def _(slot=slot):
            up_copy(slot).wait_send()

        @pl.when((mine <= slot) & (mine > 0))
        def _(slot=slot):
            down_copy(slot).wait_send()

    def drain_mate(step, peer):
        row_copy(step, my_mate, peer).wait_send()
        partial_copy(step, my_mate, peer).wait_send()

    def drain(step, peer):
        gram_copy(step, peer, my_plane).wait_send()
        gather_copy(step, my_plane, peer).wait_send()

    each_mate(drain_mate)
    each_plane_peer(drain)


def finish_kernel(root, x_ref, sums_ref, a_ref, r_ref, next_ref):
    width = a_ref.shape[0]
    corr = sums_ref[:width, :width]
    block_a = sums_ref[:width, width:]
    cross = sums_ref[width:, width:]
    a_ref[...] = block_a
    resid = x_ref[:, width:] - jnp.dot(x_ref[:, :width], block_a, precision=HIGH, preferred_element_type=F32)
    middle = jnp.dot(corr, block_a, precision=HIGH, preferred_element_type=F32) - 2.0 * block_a
    gram = cross + jnp.dot(block_a.T, middle, precision=HIGH, preferred_element_type=F32)
    row = lax.broadcasted_iota(jnp.int32, (width, width), 0)
    col = lax.broadcasted_iota(jnp.int32, (width, width), 1)
    eye = jnp.where(row == col, 1.0, 0.0)
    work = jnp.concatenate([gram, eye], axis=1)
    done = []
    for base in range(0, width, PANEL):
        lines = [work[base + i : base + i + 1, :] for i in range(PANEL)]
        sides = [jnp.broadcast_to(work[:, base + i : base + i + 1], work.shape) for i in range(PANEL)]
        pivots = {
            (i, k): jnp.broadcast_to(lines[i][:, base + k : base + k + 1], lines[i].shape)
            for i in range(PANEL)
            for k in range(i, PANEL)
        }
        change = None
        for i in range(PANEL):
            scale = lax.rsqrt(pivots[i, i])
            line = lines[i] * scale
            side = sides[i] * scale
            done.append(line)
            beta = {k: pivots[i, k] * scale for k in range(i + 1, PANEL)}
            for k in range(i + 1, PANEL):
                lines[k] = lines[k] - beta[k] * line
                sides[k] = sides[k] - beta[k] * side
                for m in range(k, PANEL):
                    pivots[k, m] = pivots[k, m] - beta[k] * beta[m]
            change = side * line if change is None else change + side * line
        work = work - change
    factor = jnp.concatenate(done, axis=0)
    r_ref[...] = jnp.where(row <= col, factor[:, :width], 0.0)
    inverse = factor[:, width:].T
    next_ref[...] = jnp.dot(resid, inverse, precision=HIGH, preferred_element_type=F32) * root


VMEM = pl.BlockSpec(memory_space=pltpu.VMEM)
SMEM = pl.BlockSpec(memory_space=pltpu.SMEM)
PARAMS = pltpu.CompilerParams(vmem_limit_bytes=48 * 1024 * 1024)


def per_device(tokens, lengths, embed, conv_w, conv_b, inv_len, hyper, probes, prev_probes, coupling):
    rows, width = prev_probes.shape
    vocab, channels = embed.shape
    taps = conv_w.shape[0]
    seq = tokens.shape[1]
    depth = taps * vocab
    cols, own_rows = pl.pallas_call(
        feature_kernel,
        out_shape=(
            jax.ShapeDtypeStruct((channels + EXTRA + width, rows), BF16),
            jax.ShapeDtypeStruct((rows, channels), BF16),
        ),
        in_specs=[VMEM] * 7,
        out_specs=(VMEM, VMEM),
        scratch_shapes=[
            pltpu.VMEM((rows, 128), jnp.int32),
            pltpu.VMEM((seq * vocab, rows), BF16),
            pltpu.VMEM((depth, channels), F32),
            pltpu.VMEM((channels, depth), BF16),
            pltpu.VMEM((channels, depth), BF16),
            pltpu.VMEM((channels, rows), F32),
        ],
        compiler_params=PARAMS,
    )(tokens, lengths.reshape(1, -1), embed, conv_w, conv_b.reshape(1, -1), inv_len.reshape(-1, 1), probes)
    line = LINE
    plane = lax.axis_size("blk") // line * lax.axis_size("rep")
    mates = plane // 2
    piece = 2 * width // plane
    dma = pltpu.SemaphoreType.DMA
    pair, sums = pl.pallas_call(
        apply_kernel,
        out_shape=(
            jax.ShapeDtypeStruct((rows, 2 * width), F32),
            jax.ShapeDtypeStruct((2 * width, 2 * width), F32),
        ),
        in_specs=[SMEM] + [VMEM] * 5,
        out_specs=(VMEM, VMEM),
        scratch_shapes=[
            pltpu.VMEM((mates, rows, channels), BF16),
            pltpu.VMEM((line, 2, channels + EXTRA + width, rows), BF16),
            pltpu.VMEM((mates, rows, 1), F32),
            pltpu.VMEM((mates, rows, width), F32),
            pltpu.VMEM((mates + 1, rows // 2, 2 * width), F32),
            pltpu.VMEM((mates, rows // 2, 2 * width), F32),
            pltpu.VMEM((plane, piece, 2 * width), F32),
            pltpu.VMEM((plane, piece, 2 * width), F32),
            pltpu.VMEM((line, piece, 2 * width), F32),
            pltpu.VMEM((plane, piece, 2 * width), F32),
            dma((mates,)),
            dma((mates,)),
            dma((line,)),
            dma((line,)),
            dma((line,)),
            dma((line,)),
            dma((line,)),
            dma((mates,)),
            dma((mates,)),
            dma((plane,)),
            dma((plane,)),
            dma((line,)),
            dma((line,)),
            dma((plane,)),
            dma((plane,)),
        ],
        compiler_params=pltpu.CompilerParams(
            vmem_limit_bytes=48 * 1024 * 1024, collective_id=0, has_side_effects=True
        ),
    )(hyper, own_rows, cols, probes, prev_probes, coupling)
    root = math.sqrt(rows * plane * line)
    return pl.pallas_call(
        functools.partial(finish_kernel, root),
        out_shape=(
            jax.ShapeDtypeStruct((width, width), F32),
            jax.ShapeDtypeStruct((width, width), F32),
            jax.ShapeDtypeStruct((rows, width), F32),
        ),
        in_specs=[VMEM] * 2,
        out_specs=(VMEM, VMEM, VMEM),
        compiler_params=PARAMS,
    )(pair, sums)


def solution(mesh):
    return jax.shard_map(
        per_device,
        mesh=mesh,
        in_specs=(
            P("blk", None),
            P("blk"),
            P(),
            P(),
            P(),
            P(),
            P(),
            P("blk", None),
            P(("blk", "rep"), None),
            P(),
        ),
        out_specs=(P(), P(), P(("blk", "rep"), None)),
        check_vma=False,
    )
```

```python
import functools
import math

import jax
import jax.numpy as jnp
from jax import lax
from jax.experimental import pallas as pl
from jax.experimental.pallas import tpu as pltpu
from jax.sharding import PartitionSpec as P

F32 = jnp.float32
BF16 = jnp.bfloat16
EXTRA = 16
LINE = 4
GROUP = 4
PANEL = 4
HIGH = lax.Precision.HIGHEST


def build_table(embed_ref, conv_w_ref, conv_b_ref, table, table_hi, table_lo):
    taps, width, channels = conv_w_ref.shape
    vocab = embed_ref.shape[0]
    groups = channels // width
    in_group = lax.broadcasted_iota(jnp.int32, (channels, channels), 0) // width
    out_group = lax.broadcasted_iota(jnp.int32, (channels, channels), 1) // width
    same = in_group == out_group
    for tap in range(taps):
        tiled = jnp.concatenate([conv_w_ref[tap].astype(F32)] * groups, axis=0)
        dense = jnp.where(same, tiled, 0.0).astype(BF16)
        entry = jnp.dot(embed_ref[...], dense, preferred_element_type=F32)
        if tap == 0:
            entry = entry + conv_b_ref[...]
        table[tap * vocab : (tap + 1) * vocab, :] = entry
    full = table[...].T
    high = full.astype(BF16)
    table_hi[...] = high
    table_lo[...] = (full - high.astype(F32)).astype(BF16)


def pooled_features(
    tokens_ref, lengths_ref, inv_len_ref, first, rows, taps, vocab, padded, onehot, table_hi, table_lo, pooled
):
    seq = tokens_ref.shape[1]
    channels = inv_len_ref.shape[0]
    positions = (seq - taps) // 2 + 1
    padded[...] = jnp.zeros_like(padded)
    padded[:, :seq] = tokens_ref[pl.ds(first, rows), :]
    token_rows = padded[...].T
    vocab_ids = lax.broadcasted_iota(jnp.int32, (vocab, rows), 0)
    for spot in range(seq):
        hit = jnp.broadcast_to(token_rows[spot : spot + 1, :], (vocab, rows)) == vocab_ids
        onehot[spot * vocab : (spot + 1) * vocab, :] = jnp.where(hit, 1.0, 0.0).astype(BF16)
    counts = (lengths_ref[:, pl.ds(first, rows)] - taps) // 2 + 1
    pooled[...] = jnp.zeros_like(pooled)
    root = math.sqrt(2.0 / math.pi)

    def position_step(group, carry):
        total = None
        for part in range(GROUP):
            position = group * GROUP + part
            start = pl.multiple_of(position * (2 * vocab), 2 * vocab)
            window = onehot[pl.ds(start, taps * vocab), :]
            preact = jnp.dot(table_hi[...], window, preferred_element_type=F32)
            preact = preact + jnp.dot(table_lo[...], window, preferred_element_type=F32)
            inner = preact * (root + (root * 0.044715) * (preact * preact))
            half = jnp.where(position < counts, 0.5, 0.0)
            weighted = preact * half
            term = weighted + weighted * jnp.tanh(inner)
            total = term if total is None else total + term
        pooled[...] += total
        return carry

    lax.fori_loop(0, positions // GROUP, position_step, 0)
    mean_pool = pooled[...] / counts.astype(F32)
    centered = mean_pool - jnp.mean(mean_pool, axis=0, keepdims=True)
    variance = jnp.mean(centered * centered, axis=0, keepdims=True)
    normed = centered * lax.rsqrt(variance + 1e-05)
    return (normed * inv_len_ref[...]).astype(BF16)


def feature_kernel(
    tokens_ref,
    lengths_ref,
    embed_ref,
    conv_w_ref,
    conv_b_ref,
    inv_len_ref,
    probes_ref,
    cols_ref,
    rows_ref,
    padded,
    onehot,
    table,
    table_hi,
    table_lo,
    pooled,
):
    rows = cols_ref.shape[1]
    channels = inv_len_ref.shape[0]
    first = pl.multiple_of(lax.axis_index("rep") * rows, rows)
    build_table(embed_ref, conv_w_ref, conv_b_ref, table, table_hi, table_lo)
    feat = pooled_features(
        tokens_ref,
        lengths_ref,
        inv_len_ref,
        first,
        rows,
        conv_w_ref.shape[0],
        embed_ref.shape[0],
        padded,
        onehot,
        table_hi,
        table_lo,
        pooled,
    )
    wide = feat.astype(F32)
    half_sq = -0.5 * jnp.sum(wide * wide, axis=0, keepdims=True)
    cols_ref[:channels, :] = feat
    high = half_sq.astype(BF16).astype(F32)
    middle = (half_sq - high).astype(BF16).astype(F32)
    low = half_sq - high - middle
    order = lax.broadcasted_iota(jnp.int32, (EXTRA, rows), 0)
    tail = jnp.where(order == 0, high, jnp.where(order == 1, middle, jnp.where(order == 2, low, 0.0)))
    cols_ref[channels : channels + EXTRA, :] = tail.astype(BF16)
    cols_ref[channels + EXTRA :, :] = probes_ref[pl.ds(first, rows), :].astype(F32).T.astype(BF16)
    rows_ref[...] = wide.T.astype(BF16)


def apply_kernel(
    hyper_ref,
    rows_ref,
    cols_ref,
    own_ref,
    prev_ref,
    coupling_ref,
    x_ref,
    sums_ref,
    row_blocks,
    col_blocks,
    row_halves,
    totals,
    partial_out,
    partial_in,
    gram_out,
    gram_in,
    line_in,
    gathered,
    row_send,
    row_recv,
    col_send,
    col_recv,
    side_send,
    side_recv,
    partial_send,
    partial_recv,
    gram_send,
    gram_recv,
    line_send,
    line_recv,
    gather_send,
    gather_recv,
):
    rows, channels = rows_ref.shape
    mates = row_blocks.shape[0]
    line = col_blocks.shape[0]
    plane = gram_out.shape[0]
    width = prev_ref.shape[1]
    reps = lax.axis_size("rep")
    low = plane // reps
    blk = lax.axis_index("blk")
    rep = lax.axis_index("rep")
    core = lax.rem(blk, 2)
    other = 1 - core
    mine = blk // low
    my_plane = lax.rem(blk, low) * reps + rep
    my_mate = (lax.rem(blk, low) // 2) * reps + rep

    def plane_id(spot):
        return {"blk": mine * low + spot // reps, "rep": lax.rem(spot, reps)}

    def mate_id(spot):
        return {"blk": mine * low + (spot // reps) * 2 + core, "rep": lax.rem(spot, reps)}

    def line_id(spot):
        return {"blk": spot * low + lax.rem(blk, low), "rep": rep}

    sibling = {"blk": blk + 1 - 2 * core, "rep": rep}

    def plane_peer(step):
        return lax.rem(my_plane + step, plane)

    def mate_peer(step):
        return lax.rem(my_mate + step, mates)

    line_peers = [mine, mine + 1 - 2 * lax.rem(mine, 2), lax.rem(mine + 2, 4), 3 - mine]

    def copy(src, dst, send_sem, recv_sem, device):
        return pltpu.make_async_remote_copy(
            src_ref=src,
            dst_ref=dst,
            send_sem=send_sem,
            recv_sem=recv_sem,
            device_id=device,
            device_id_type=pl.DeviceIdType.MESH,
        )

    def each_plane_peer(action):
        def body(step, carry):
            action(step, plane_peer(step))
            return carry

        lax.fori_loop(1, plane, body, 0)

    def each_mate(action):
        def body(step, carry):
            action(step, mate_peer(step))
            return carry

        lax.fori_loop(1, mates, body, 0)

    barrier = pltpu.get_barrier_semaphore()

    def greet(step, peer):
        pl.semaphore_signal(barrier, inc=1, device_id=plane_id(peer), device_id_type=pl.DeviceIdType.MESH)

    each_plane_peer(greet)
    for peer in line_peers[1:]:
        pl.semaphore_signal(barrier, inc=1, device_id=line_id(peer), device_id_type=pl.DeviceIdType.MESH)
    pl.semaphore_wait(barrier, plane - 1 + line - 1)

    def col_copy(order, slot, peer):
        return copy(cols_ref, col_blocks.at[slot, core], col_send.at[order], col_recv.at[slot], line_id(peer))

    def side_copy(slot, lane, src=None):
        src = col_blocks.at[slot, lane] if src is None else src
        return copy(src, col_blocks.at[slot, lane], side_send.at[slot], side_recv.at[slot], sibling)

    def row_copy(step, slot, peer):
        return copy(rows_ref, row_blocks.at[slot], row_send.at[step], row_recv.at[slot], mate_id(peer))

    col_copy(1, mine, line_peers[1]).start()
    each_mate(lambda step, peer: row_copy(step, my_mate, peer).start())
    col_copy(2, mine, line_peers[2]).start()
    col_copy(3, mine, line_peers[3]).start()
    side_copy(mine, core, cols_ref).start()
    row_blocks[my_mate] = rows_ref[...]
    col_blocks[mine, core] = cols_ref[...]
    amplitude = hyper_ref[0]

    def partial_copy(step, slot, peer):
        return copy(
            partial_out.at[step], partial_in.at[slot], partial_send.at[step], partial_recv.at[slot], mate_id(peer)
        )

    def packed(value):
        return jnp.concatenate([value[: rows // 2, :], value[rows // 2 :, :]], axis=1)

    def column_pass(source, order):
        if order:
            col_copy(order, source, source).wait_recv()
            side_copy(source, core).start()
        side_copy(source, other).wait_recv()
        parts = []
        for lane in range(2):
            cols = col_blocks.at[source, lane]
            col_half = jnp.sum(cols[channels : channels + EXTRA, :].astype(F32), axis=0, keepdims=True)
            block_probes = cols[channels + EXTRA :, :].astype(F32).T.astype(BF16)
            parts.append((cols, col_half, block_probes))
        last = order == line - 1

        group = 1 if order == 0 else 2

        def pair_step(pair, carry):
            steps = [group * pair + part + (1 if last else 0) for part in range(group)]
            if order == 0:
                for step in steps:
                    spot = mate_peer(step)

                    @pl.when(step > 0)
                    def _():
                        row_copy(step, spot, spot).wait_recv()

                    wide = row_blocks[spot].astype(F32)
                    row_halves[spot] = -0.5 * jnp.sum(wide * wide, axis=1, keepdims=True)
            for step in steps:
                spot = mate_peer(step)
                value = None if order == 0 else totals[spot]
                for cols, col_half, block_probes in parts:
                    inner = jnp.dot(row_blocks[spot], cols[:channels, :], preferred_element_type=F32)
                    exponent = jnp.minimum(inner + (row_halves[spot] + col_half), 0.0)
                    weights = (amplitude * jnp.exp(exponent)).astype(BF16)
                    term = jnp.dot(weights, block_probes, preferred_element_type=F32)
                    value = term if value is None else value + term
                if last:
                    partial_out[step] = packed(value)
                else:
                    totals[spot] = value
            if last:
                for step in steps:
                    spot = mate_peer(step)

                    @pl.when(step < mates)
                    def _():
                        partial_copy(step, my_mate, spot).start()

            return carry

        lax.fori_loop(0, mates // group, pair_step, 0)

    for order in range(line):
        column_pass(line_peers[order], order)

    own = own_ref[pl.ds(pl.multiple_of(rep * rows, rows), rows), :].astype(F32)
    root = 1.0 / math.sqrt(rows * plane * line)
    coupled = lax.dot_general(
        prev_ref[...].astype(F32),
        coupling_ref[...],
        (((1,), (1,)), ((), ())),
        precision=HIGH,
        preferred_element_type=F32,
    )

    def add_partial(step, total):
        spot = mate_peer(step)
        partial_copy(step, spot, spot).wait_recv()
        return total + partial_in[spot]

    total = lax.fori_loop(1, mates, add_partial, partial_out[mates])
    applied = jnp.concatenate([total[:, :width], total[:, width:]], axis=0)
    x_ref[:, :width] = own * root
    x_ref[:, width:] = (applied + hyper_ref[1] * own - coupled) * root
    both = x_ref[...]
    gram = jnp.dot(both.T, both, precision=HIGH, preferred_element_type=F32)
    piece = gram_out.shape[1]
    for spot in range(plane):
        gram_out[spot] = gram[spot * piece : (spot + 1) * piece, :]

    def gram_copy(step, target, slot):
        return copy(gram_out.at[target], gram_in.at[slot], gram_send.at[step], gram_recv.at[slot], plane_id(target))

    each_plane_peer(lambda step, peer: gram_copy(step, peer, my_plane).start())

    def add_gram(step, total):
        spot = plane_peer(step)
        gram_copy(step, spot, spot).wait_recv()
        return total + gram_in[spot]

    line_in[mine] = lax.fori_loop(1, plane, add_gram, gram_out[my_plane])

    def line_copy(order, slot, peer):
        return copy(line_in.at[mine], line_in.at[slot], line_send.at[order], line_recv.at[slot], line_id(peer))

    for order in range(1, line):
        line_copy(order, mine, line_peers[order]).start()
    for order in range(1, line):
        line_copy(order, line_peers[order], line_peers[order]).wait_recv()
    gathered[my_plane] = (line_in[0] + line_in[1]) + (line_in[2] + line_in[3])

    def gather_copy(step, slot, peer):
        return copy(
            gathered.at[my_plane], gathered.at[slot], gather_send.at[step], gather_recv.at[slot], plane_id(peer)
        )

    each_plane_peer(lambda step, peer: gather_copy(step, my_plane, peer).start())
    each_plane_peer(lambda step, peer: gather_copy(step, peer, peer).wait_recv())
    for spot in range(plane):
        sums_ref[spot * piece : (spot + 1) * piece, :] = gathered[spot]
    for order in range(1, line):
        line_copy(order, mine, line_peers[order]).wait_send()
        col_copy(order, mine, line_peers[order]).wait_send()
    for slot in range(line):
        side_copy(slot, core).wait_send()

    def drain_mate(step, peer):
        row_copy(step, my_mate, peer).wait_send()
        partial_copy(step, my_mate, peer).wait_send()

    def drain(step, peer):
        gram_copy(step, peer, my_plane).wait_send()
        gather_copy(step, my_plane, peer).wait_send()

    each_mate(drain_mate)
    each_plane_peer(drain)


def finish_kernel(root, x_ref, sums_ref, a_ref, r_ref, next_ref):
    width = a_ref.shape[0]
    corr = sums_ref[:width, :width]
    block_a = sums_ref[:width, width:]
    cross = sums_ref[width:, width:]
    a_ref[...] = block_a
    resid = x_ref[:, width:] - jnp.dot(x_ref[:, :width], block_a, precision=HIGH, preferred_element_type=F32)
    middle = jnp.dot(corr, block_a, precision=HIGH, preferred_element_type=F32) - 2.0 * block_a
    gram = cross + jnp.dot(block_a.T, middle, precision=HIGH, preferred_element_type=F32)
    row = lax.broadcasted_iota(jnp.int32, (width, width), 0)
    col = lax.broadcasted_iota(jnp.int32, (width, width), 1)
    eye = jnp.where(row == col, 1.0, 0.0)
    work = jnp.concatenate([gram, eye], axis=1)
    done = []
    for base in range(0, width, PANEL):
        lines = [work[base + i : base + i + 1, :] for i in range(PANEL)]
        sides = [jnp.broadcast_to(work[:, base + i : base + i + 1], work.shape) for i in range(PANEL)]
        pivots = {
            (i, k): jnp.broadcast_to(lines[i][:, base + k : base + k + 1], lines[i].shape)
            for i in range(PANEL)
            for k in range(i, PANEL)
        }
        change = None
        for i in range(PANEL):
            scale = lax.rsqrt(pivots[i, i])
            line = lines[i] * scale
            side = sides[i] * scale
            done.append(line)
            beta = {k: pivots[i, k] * scale for k in range(i + 1, PANEL)}
            for k in range(i + 1, PANEL):
                lines[k] = lines[k] - beta[k] * line
                sides[k] = sides[k] - beta[k] * side
                for m in range(k, PANEL):
                    pivots[k, m] = pivots[k, m] - beta[k] * beta[m]
            change = side * line if change is None else change + side * line
        work = work - change
    factor = jnp.concatenate(done, axis=0)
    r_ref[...] = jnp.where(row <= col, factor[:, :width], 0.0)
    inverse = factor[:, width:].T
    next_ref[...] = jnp.dot(resid, inverse, precision=HIGH, preferred_element_type=F32) * root


VMEM = pl.BlockSpec(memory_space=pltpu.VMEM)
SMEM = pl.BlockSpec(memory_space=pltpu.SMEM)
PARAMS = pltpu.CompilerParams(vmem_limit_bytes=48 * 1024 * 1024)


def per_device(tokens, lengths, embed, conv_w, conv_b, inv_len, hyper, probes, prev_probes, coupling):
    rows, width = prev_probes.shape
    vocab, channels = embed.shape
    taps = conv_w.shape[0]
    seq = tokens.shape[1]
    depth = taps * vocab
    cols, own_rows = pl.pallas_call(
        feature_kernel,
        out_shape=(
            jax.ShapeDtypeStruct((channels + EXTRA + width, rows), BF16),
            jax.ShapeDtypeStruct((rows, channels), BF16),
        ),
        in_specs=[VMEM] * 7,
        out_specs=(VMEM, VMEM),
        scratch_shapes=[
            pltpu.VMEM((rows, 128), jnp.int32),
            pltpu.VMEM((seq * vocab, rows), BF16),
            pltpu.VMEM((depth, channels), F32),
            pltpu.VMEM((channels, depth), BF16),
            pltpu.VMEM((channels, depth), BF16),
            pltpu.VMEM((channels, rows), F32),
        ],
        compiler_params=PARAMS,
    )(tokens, lengths.reshape(1, -1), embed, conv_w, conv_b.reshape(1, -1), inv_len.reshape(-1, 1), probes)
    line = LINE
    plane = lax.axis_size("blk") // line * lax.axis_size("rep")
    mates = plane // 2
    piece = 2 * width // plane
    dma = pltpu.SemaphoreType.DMA
    pair, sums = pl.pallas_call(
        apply_kernel,
        out_shape=(
            jax.ShapeDtypeStruct((rows, 2 * width), F32),
            jax.ShapeDtypeStruct((2 * width, 2 * width), F32),
        ),
        in_specs=[SMEM] + [VMEM] * 5,
        out_specs=(VMEM, VMEM),
        scratch_shapes=[
            pltpu.VMEM((mates, rows, channels), BF16),
            pltpu.VMEM((line, 2, channels + EXTRA + width, rows), BF16),
            pltpu.VMEM((mates, rows, 1), F32),
            pltpu.VMEM((mates, rows, width), F32),
            pltpu.VMEM((mates + 1, rows // 2, 2 * width), F32),
            pltpu.VMEM((mates, rows // 2, 2 * width), F32),
            pltpu.VMEM((plane, piece, 2 * width), F32),
            pltpu.VMEM((plane, piece, 2 * width), F32),
            pltpu.VMEM((line, piece, 2 * width), F32),
            pltpu.VMEM((plane, piece, 2 * width), F32),
            dma((mates,)),
            dma((mates,)),
            dma((line,)),
            dma((line,)),
            dma((line,)),
            dma((line,)),
            dma((mates,)),
            dma((mates,)),
            dma((plane,)),
            dma((plane,)),
            dma((line,)),
            dma((line,)),
            dma((plane,)),
            dma((plane,)),
        ],
        compiler_params=pltpu.CompilerParams(
            vmem_limit_bytes=48 * 1024 * 1024, collective_id=0, has_side_effects=True
        ),
    )(hyper, own_rows, cols, probes, prev_probes, coupling)
    root = math.sqrt(rows * plane * line)
    return pl.pallas_call(
        functools.partial(finish_kernel, root),
        out_shape=(
            jax.ShapeDtypeStruct((width, width), F32),
            jax.ShapeDtypeStruct((width, width), F32),
            jax.ShapeDtypeStruct((rows, width), F32),
        ),
        in_specs=[VMEM] * 2,
        out_specs=(VMEM, VMEM, VMEM),
        compiler_params=PARAMS,
    )(pair, sums)


def solution(mesh):
    return jax.shard_map(
        per_device,
        mesh=mesh,
        in_specs=(
            P("blk", None),
            P("blk"),
            P(),
            P(),
            P(),
            P(),
            P(),
            P("blk", None),
            P(("blk", "rep"), None),
            P(),
        ),
        out_specs=(P(), P(), P(("blk", "rep"), None)),
        check_vma=False,
    )
```

```python
import functools
import math

import jax
import jax.numpy as jnp
from jax import lax
from jax.experimental import pallas as pl
from jax.experimental.pallas import tpu as pltpu
from jax.sharding import PartitionSpec as P

F32 = jnp.float32
BF16 = jnp.bfloat16
EXTRA = 16
LINE = 4
GROUP = 4
PANEL = 4
HIGH = lax.Precision.HIGHEST


def build_table(embed_ref, conv_w_ref, conv_b_ref, table, table_hi, table_lo):
    taps, width, channels = conv_w_ref.shape
    vocab = embed_ref.shape[0]
    groups = channels // width
    in_group = lax.broadcasted_iota(jnp.int32, (channels, channels), 0) // width
    out_group = lax.broadcasted_iota(jnp.int32, (channels, channels), 1) // width
    same = in_group == out_group
    for tap in range(taps):
        tiled = jnp.concatenate([conv_w_ref[tap].astype(F32)] * groups, axis=0)
        dense = jnp.where(same, tiled, 0.0).astype(BF16)
        entry = jnp.dot(embed_ref[...], dense, preferred_element_type=F32)
        if tap == 0:
            entry = entry + conv_b_ref[...]
        table[tap * vocab : (tap + 1) * vocab, :] = entry
    full = table[...].T
    high = full.astype(BF16)
    table_hi[...] = high
    table_lo[...] = (full - high.astype(F32)).astype(BF16)


def pooled_features(
    tokens_ref, lengths_ref, inv_len_ref, first, rows, taps, vocab, padded, onehot, table_hi, table_lo, pooled
):
    seq = tokens_ref.shape[1]
    channels = inv_len_ref.shape[0]
    positions = (seq - taps) // 2 + 1
    padded[...] = jnp.zeros_like(padded)
    padded[:, :seq] = tokens_ref[pl.ds(first, rows), :]
    token_rows = padded[...].T
    vocab_ids = lax.broadcasted_iota(jnp.int32, (vocab, rows), 0)
    for spot in range(seq):
        hit = jnp.broadcast_to(token_rows[spot : spot + 1, :], (vocab, rows)) == vocab_ids
        onehot[spot * vocab : (spot + 1) * vocab, :] = jnp.where(hit, 1.0, 0.0).astype(BF16)
    counts = (lengths_ref[:, pl.ds(first, rows)] - taps) // 2 + 1
    pooled[...] = jnp.zeros_like(pooled)
    root = math.sqrt(2.0 / math.pi)

    def position_step(group, carry):
        total = None
        for part in range(GROUP):
            position = group * GROUP + part
            start = pl.multiple_of(position * (2 * vocab), 2 * vocab)
            window = onehot[pl.ds(start, taps * vocab), :]
            preact = jnp.dot(table_hi[...], window, preferred_element_type=F32)
            preact = preact + jnp.dot(table_lo[...], window, preferred_element_type=F32)
            inner = preact * (root + (root * 0.044715) * (preact * preact))
            half = jnp.where(position < counts, 0.5, 0.0)
            weighted = preact * half
            term = weighted + weighted * jnp.tanh(inner)
            total = term if total is None else total + term
        pooled[...] += total
        return carry

    lax.fori_loop(0, positions // GROUP, position_step, 0)
    mean_pool = pooled[...] / counts.astype(F32)
    centered = mean_pool - jnp.mean(mean_pool, axis=0, keepdims=True)
    variance = jnp.mean(centered * centered, axis=0, keepdims=True)
    normed = centered * lax.rsqrt(variance + 1e-05)
    return (normed * inv_len_ref[...]).astype(BF16)


def feature_kernel(
    tokens_ref,
    lengths_ref,
    embed_ref,
    conv_w_ref,
    conv_b_ref,
    inv_len_ref,
    cols_ref,
    rows_ref,
    padded,
    onehot,
    table,
    table_hi,
    table_lo,
    pooled,
):
    rows = cols_ref.shape[1]
    channels = inv_len_ref.shape[0]
    first = pl.multiple_of(lax.axis_index("rep") * rows, rows)
    build_table(embed_ref, conv_w_ref, conv_b_ref, table, table_hi, table_lo)
    feat = pooled_features(
        tokens_ref,
        lengths_ref,
        inv_len_ref,
        first,
        rows,
        conv_w_ref.shape[0],
        embed_ref.shape[0],
        padded,
        onehot,
        table_hi,
        table_lo,
        pooled,
    )
    wide = feat.astype(F32)
    half_sq = -0.5 * jnp.sum(wide * wide, axis=0, keepdims=True)
    cols_ref[:channels, :] = feat
    high = half_sq.astype(BF16).astype(F32)
    middle = (half_sq - high).astype(BF16).astype(F32)
    low = half_sq - high - middle
    order = lax.broadcasted_iota(jnp.int32, (EXTRA, rows), 0)
    tail = jnp.where(order == 0, high, jnp.where(order == 1, middle, jnp.where(order == 2, low, 0.0)))
    cols_ref[channels : channels + EXTRA, :] = tail.astype(BF16)
    rows_ref[...] = wide.T.astype(BF16)


def apply_kernel(
    hyper_ref,
    tokens_ref,
    lengths_ref,
    embed_ref,
    conv_w_ref,
    conv_b_ref,
    inv_len_ref,
    own_ref,
    prev_ref,
    coupling_ref,
    x_ref,
    sums_ref,
    cols_ref,
    rows_ref,
    padded,
    onehot,
    table,
    table_hi,
    table_lo,
    pooled,
    probe_blocks,
    probe_send,
    probe_recv,
    share_send,
    share_recv,
    row_blocks,
    col_blocks,
    row_halves,
    totals,
    partial_out,
    partial_in,
    gram_out,
    gram_in,
    line_in,
    gathered,
    row_send,
    row_recv,
    col_send,
    col_recv,
    side_send,
    side_recv,
    partial_send,
    partial_recv,
    gram_send,
    gram_recv,
    line_send,
    line_recv,
    gather_send,
    gather_recv,
):
    rows, channels = rows_ref.shape
    mates = row_blocks.shape[0]
    line = col_blocks.shape[0]
    plane = gram_out.shape[0]
    width = prev_ref.shape[1]
    reps = lax.axis_size("rep")
    low = plane // reps
    blk = lax.axis_index("blk")
    rep = lax.axis_index("rep")
    core = lax.rem(blk, 2)
    other = 1 - core
    mine = blk // low
    my_plane = lax.rem(blk, low) * reps + rep
    my_mate = (lax.rem(blk, low) // 2) * reps + rep

    def plane_id(spot):
        return {"blk": mine * low + spot // reps, "rep": lax.rem(spot, reps)}

    def mate_id(spot):
        return {"blk": mine * low + (spot // reps) * 2 + core, "rep": lax.rem(spot, reps)}

    def line_id(spot):
        return {"blk": spot * low + lax.rem(blk, low), "rep": rep}

    sibling = {"blk": blk + 1 - 2 * core, "rep": rep}

    def plane_peer(step):
        return lax.rem(my_plane + step, plane)

    def mate_peer(step):
        return lax.rem(my_mate + step, mates)

    line_peers = [mine, mine + 1 - 2 * lax.rem(mine, 2), lax.rem(mine + 2, 4), 3 - mine]

    def copy(src, dst, send_sem, recv_sem, device):
        return pltpu.make_async_remote_copy(
            src_ref=src,
            dst_ref=dst,
            send_sem=send_sem,
            recv_sem=recv_sem,
            device_id=device,
            device_id_type=pl.DeviceIdType.MESH,
        )

    def each_plane_peer(action):
        def body(step, carry):
            action(step, plane_peer(step))
            return carry

        lax.fori_loop(1, plane, body, 0)

    def each_mate(action):
        def body(step, carry):
            action(step, mate_peer(step))
            return carry

        lax.fori_loop(1, mates, body, 0)

    barrier = pltpu.get_barrier_semaphore()

    def greet(step, peer):
        pl.semaphore_signal(barrier, inc=1, device_id=plane_id(peer), device_id_type=pl.DeviceIdType.MESH)

    each_plane_peer(greet)
    for peer in line_peers[1:]:
        pl.semaphore_signal(barrier, inc=1, device_id=line_id(peer), device_id_type=pl.DeviceIdType.MESH)
    own = own_ref[pl.ds(pl.multiple_of(rep * rows, rows), rows), :].astype(F32)
    probe_blocks[core, mine] = own.T.astype(BF16)
    pl.semaphore_wait(barrier, plane - 1 + line - 1)

    def probe_copy(order, slot, peer):
        return copy(
            probe_blocks.at[core, mine],
            probe_blocks.at[core, slot],
            probe_send.at[order],
            probe_recv.at[slot],
            line_id(peer),
        )

    def share_copy(lane):
        return copy(probe_blocks.at[lane], probe_blocks.at[lane], share_send.at[0], share_recv.at[0], sibling)

    for order in range(1, line):
        probe_copy(order, mine, line_peers[order]).start()
    feature_kernel(
        tokens_ref,
        lengths_ref,
        embed_ref,
        conv_w_ref,
        conv_b_ref,
        inv_len_ref,
        cols_ref,
        rows_ref,
        padded,
        onehot,
        table,
        table_hi,
        table_lo,
        pooled,
    )

    def col_copy(order, slot, peer):
        return copy(cols_ref, col_blocks.at[slot, core], col_send.at[order], col_recv.at[slot], line_id(peer))

    def side_copy(slot, lane, src=None):
        src = col_blocks.at[slot, lane] if src is None else src
        return copy(src, col_blocks.at[slot, lane], side_send.at[slot], side_recv.at[slot], sibling)

    def row_copy(step, slot, peer):
        return copy(rows_ref, row_blocks.at[slot], row_send.at[step], row_recv.at[slot], mate_id(peer))

    col_copy(1, mine, line_peers[1]).start()
    each_mate(lambda step, peer: row_copy(step, my_mate, peer).start())
    col_copy(2, mine, line_peers[2]).start()
    col_copy(3, mine, line_peers[3]).start()
    side_copy(mine, core, cols_ref).start()
    row_blocks[my_mate] = rows_ref[...]
    col_blocks[mine, core] = cols_ref[...]
    amplitude = hyper_ref[0]
    for order in range(1, line):
        probe_copy(order, line_peers[order], line_peers[order]).wait_recv()
    share_copy(core).start()
    root = 1.0 / math.sqrt(rows * plane * line)
    coupled = lax.dot_general(
        prev_ref[...].astype(F32),
        coupling_ref[...],
        (((1,), (1,)), ((), ())),
        precision=HIGH,
        preferred_element_type=F32,
    )
    x_ref[:, :width] = own * root
    x_ref[:, width:] = (hyper_ref[1] * own - coupled) * root
    share_copy(other).wait_recv()

    def partial_copy(step, slot, peer):
        return copy(
            partial_out.at[step], partial_in.at[slot], partial_send.at[step], partial_recv.at[slot], mate_id(peer)
        )

    def packed(value):
        return jnp.concatenate([value[: rows // 2, :], value[rows // 2 :, :]], axis=1)

    def column_pass(source, order):
        if order:
            col_copy(order, source, source).wait_recv()
            side_copy(source, core).start()
        side_copy(source, other).wait_recv()
        parts = []
        for lane in range(2):
            cols = col_blocks.at[source, lane]
            col_half = jnp.sum(cols[channels : channels + EXTRA, :].astype(F32), axis=0, keepdims=True)
            block_probes = probe_blocks[lane, source].astype(F32).T.astype(BF16)
            parts.append((cols, col_half, block_probes))
        last = order == line - 1

        group = 1 if order == 0 else 2

        def pair_step(pair, carry):
            steps = [group * pair + part + (1 if last else 0) for part in range(group)]
            if order == 0:
                for step in steps:
                    spot = mate_peer(step)

                    @pl.when(step > 0)
                    def _():
                        row_copy(step, spot, spot).wait_recv()

                    wide = row_blocks[spot].astype(F32)
                    row_halves[spot] = -0.5 * jnp.sum(wide * wide, axis=1, keepdims=True)
            for step in steps:
                spot = mate_peer(step)
                value = None if order == 0 else totals[spot]
                for cols, col_half, block_probes in parts:
                    inner = jnp.dot(row_blocks[spot], cols[:channels, :], preferred_element_type=F32)
                    exponent = jnp.minimum(inner + (row_halves[spot] + col_half), 0.0)
                    weights = (amplitude * jnp.exp(exponent)).astype(BF16)
                    term = jnp.dot(weights, block_probes, preferred_element_type=F32)
                    value = term if value is None else value + term
                if last:
                    partial_out[step] = packed(value)
                else:
                    totals[spot] = value
            if last:
                for step in steps:
                    spot = mate_peer(step)

                    @pl.when(step < mates)
                    def _():
                        partial_copy(step, my_mate, spot).start()

            return carry

        lax.fori_loop(0, mates // group, pair_step, 0)

    for order in range(line):
        column_pass(line_peers[order], order)

    def add_partial(step, total):
        spot = mate_peer(step)
        partial_copy(step, spot, spot).wait_recv()
        return total + partial_in[spot]

    total = lax.fori_loop(1, mates, add_partial, partial_out[mates])
    applied = jnp.concatenate([total[:, :width], total[:, width:]], axis=0)
    x_ref[:, width:] += applied * root
    both = x_ref[...]
    gram = jnp.dot(both.T, both, precision=HIGH, preferred_element_type=F32)
    piece = gram_out.shape[1]
    for spot in range(plane):
        gram_out[spot] = gram[spot * piece : (spot + 1) * piece, :]

    def gram_copy(step, target, slot):
        return copy(gram_out.at[target], gram_in.at[slot], gram_send.at[step], gram_recv.at[slot], plane_id(target))

    each_plane_peer(lambda step, peer: gram_copy(step, peer, my_plane).start())

    def add_gram(step, total):
        spot = plane_peer(step)
        gram_copy(step, spot, spot).wait_recv()
        return total + gram_in[spot]

    line_in[mine] = lax.fori_loop(1, plane, add_gram, gram_out[my_plane])

    def line_copy(order, slot, peer):
        return copy(line_in.at[mine], line_in.at[slot], line_send.at[order], line_recv.at[slot], line_id(peer))

    for order in range(1, line):
        line_copy(order, mine, line_peers[order]).start()
    for order in range(1, line):
        line_copy(order, line_peers[order], line_peers[order]).wait_recv()
    gathered[my_plane] = (line_in[0] + line_in[1]) + (line_in[2] + line_in[3])

    def gather_copy(step, slot, peer):
        return copy(
            gathered.at[my_plane], gathered.at[slot], gather_send.at[step], gather_recv.at[slot], plane_id(peer)
        )

    each_plane_peer(lambda step, peer: gather_copy(step, my_plane, peer).start())
    each_plane_peer(lambda step, peer: gather_copy(step, peer, peer).wait_recv())
    for spot in range(plane):
        sums_ref[spot * piece : (spot + 1) * piece, :] = gathered[spot]
    for order in range(1, line):
        line_copy(order, mine, line_peers[order]).wait_send()
        col_copy(order, mine, line_peers[order]).wait_send()
        probe_copy(order, mine, line_peers[order]).wait_send()
    share_copy(core).wait_send()
    for slot in range(line):
        side_copy(slot, core).wait_send()

    def drain_mate(step, peer):
        row_copy(step, my_mate, peer).wait_send()
        partial_copy(step, my_mate, peer).wait_send()

    def drain(step, peer):
        gram_copy(step, peer, my_plane).wait_send()
        gather_copy(step, my_plane, peer).wait_send()

    each_mate(drain_mate)
    each_plane_peer(drain)


def finish_kernel(root, x_ref, sums_ref, a_ref, r_ref, next_ref):
    width = a_ref.shape[0]
    corr = sums_ref[:width, :width]
    block_a = sums_ref[:width, width:]
    cross = sums_ref[width:, width:]
    a_ref[...] = block_a
    resid = x_ref[:, width:] - jnp.dot(x_ref[:, :width], block_a, precision=HIGH, preferred_element_type=F32)
    middle = jnp.dot(corr, block_a, precision=HIGH, preferred_element_type=F32) - 2.0 * block_a
    gram = cross + jnp.dot(block_a.T, middle, precision=HIGH, preferred_element_type=F32)
    row = lax.broadcasted_iota(jnp.int32, (width, width), 0)
    col = lax.broadcasted_iota(jnp.int32, (width, width), 1)
    eye = jnp.where(row == col, 1.0, 0.0)
    work = jnp.concatenate([gram, eye], axis=1)
    done = []
    for base in range(0, width, PANEL):
        lines = [work[base + i : base + i + 1, :] for i in range(PANEL)]
        sides = [jnp.broadcast_to(work[:, base + i : base + i + 1], work.shape) for i in range(PANEL)]
        pivots = {
            (i, k): jnp.broadcast_to(lines[i][:, base + k : base + k + 1], lines[i].shape)
            for i in range(PANEL)
            for k in range(i, PANEL)
        }
        change = None
        for i in range(PANEL):
            scale = lax.rsqrt(pivots[i, i])
            line = lines[i] * scale
            side = sides[i] * scale
            done.append(line)
            beta = {k: pivots[i, k] * scale for k in range(i + 1, PANEL)}
            for k in range(i + 1, PANEL):
                lines[k] = lines[k] - beta[k] * line
                sides[k] = sides[k] - beta[k] * side
                for m in range(k, PANEL):
                    pivots[k, m] = pivots[k, m] - beta[k] * beta[m]
            change = side * line if change is None else change + side * line
        work = work - change
    factor = jnp.concatenate(done, axis=0)
    r_ref[...] = jnp.where(row <= col, factor[:, :width], 0.0)
    inverse = factor[:, width:].T
    next_ref[...] = jnp.dot(resid, inverse, precision=HIGH, preferred_element_type=F32) * root


VMEM = pl.BlockSpec(memory_space=pltpu.VMEM)
SMEM = pl.BlockSpec(memory_space=pltpu.SMEM)
PARAMS = pltpu.CompilerParams(vmem_limit_bytes=48 * 1024 * 1024)


def per_device(tokens, lengths, embed, conv_w, conv_b, inv_len, hyper, probes, prev_probes, coupling):
    rows, width = prev_probes.shape
    vocab, channels = embed.shape
    taps = conv_w.shape[0]
    seq = tokens.shape[1]
    depth = taps * vocab
    line = LINE
    plane = lax.axis_size("blk") // line * lax.axis_size("rep")
    mates = plane // 2
    piece = 2 * width // plane
    dma = pltpu.SemaphoreType.DMA
    pair, sums = pl.pallas_call(
        apply_kernel,
        out_shape=(
            jax.ShapeDtypeStruct((rows, 2 * width), F32),
            jax.ShapeDtypeStruct((2 * width, 2 * width), F32),
        ),
        in_specs=[SMEM] + [VMEM] * 9,
        out_specs=(VMEM, VMEM),
        scratch_shapes=[
            pltpu.VMEM((channels + EXTRA, rows), BF16),
            pltpu.VMEM((rows, channels), BF16),
            pltpu.VMEM((rows, 128), jnp.int32),
            pltpu.VMEM((seq * vocab, rows), BF16),
            pltpu.VMEM((depth, channels), F32),
            pltpu.VMEM((channels, depth), BF16),
            pltpu.VMEM((channels, depth), BF16),
            pltpu.VMEM((channels, rows), F32),
            pltpu.VMEM((2, line, width, rows), BF16),
            dma((line,)),
            dma((line,)),
            dma((1,)),
            dma((1,)),
            pltpu.VMEM((mates, rows, channels), BF16),
            pltpu.VMEM((line, 2, channels + EXTRA, rows), BF16),
            pltpu.VMEM((mates, rows, 1), F32),
            pltpu.VMEM((mates, rows, width), F32),
            pltpu.VMEM((mates + 1, rows // 2, 2 * width), F32),
            pltpu.VMEM((mates, rows // 2, 2 * width), F32),
            pltpu.VMEM((plane, piece, 2 * width), F32),
            pltpu.VMEM((plane, piece, 2 * width), F32),
            pltpu.VMEM((line, piece, 2 * width), F32),
            pltpu.VMEM((plane, piece, 2 * width), F32),
            dma((mates,)),
            dma((mates,)),
            dma((line,)),
            dma((line,)),
            dma((line,)),
            dma((line,)),
            dma((mates,)),
            dma((mates,)),
            dma((plane,)),
            dma((plane,)),
            dma((line,)),
            dma((line,)),
            dma((plane,)),
            dma((plane,)),
        ],
        compiler_params=pltpu.CompilerParams(
            vmem_limit_bytes=48 * 1024 * 1024, collective_id=0, has_side_effects=True
        ),
    )(
        hyper,
        tokens,
        lengths.reshape(1, -1),
        embed,
        conv_w,
        conv_b.reshape(1, -1),
        inv_len.reshape(-1, 1),
        probes,
        prev_probes,
        coupling,
    )
    root = math.sqrt(rows * plane * line)
    return pl.pallas_call(
        functools.partial(finish_kernel, root),
        out_shape=(
            jax.ShapeDtypeStruct((width, width), F32),
            jax.ShapeDtypeStruct((width, width), F32),
            jax.ShapeDtypeStruct((rows, width), F32),
        ),
        in_specs=[VMEM] * 2,
        out_specs=(VMEM, VMEM, VMEM),
        compiler_params=PARAMS,
    )(pair, sums)


def solution(mesh):
    return jax.shard_map(
        per_device,
        mesh=mesh,
        in_specs=(
            P("blk", None),
            P("blk"),
            P(),
            P(),
            P(),
            P(),
            P(),
            P("blk", None),
            P(("blk", "rep"), None),
            P(),
        ),
        out_specs=(P(), P(), P(("blk", "rep"), None)),
        check_vma=False,
    )
```

```python
import functools
import math

import jax
import jax.numpy as jnp
from jax import lax
from jax.experimental import pallas as pl
from jax.experimental.pallas import tpu as pltpu
from jax.sharding import PartitionSpec as P

F32 = jnp.float32
BF16 = jnp.bfloat16
EXTRA = 16
LINE = 4
GROUP = 4
PANEL = 4
HIGH = lax.Precision.HIGHEST


def build_table(embed_ref, conv_w_ref, conv_b_ref, table, table_hi, table_lo):
    taps, width, channels = conv_w_ref.shape
    vocab = embed_ref.shape[0]
    groups = channels // width
    in_group = lax.broadcasted_iota(jnp.int32, (channels, channels), 0) // width
    out_group = lax.broadcasted_iota(jnp.int32, (channels, channels), 1) // width
    same = in_group == out_group
    for tap in range(taps):
        tiled = jnp.concatenate([conv_w_ref[tap].astype(F32)] * groups, axis=0)
        dense = jnp.where(same, tiled, 0.0).astype(BF16)
        entry = jnp.dot(embed_ref[...], dense, preferred_element_type=F32)
        if tap == 0:
            entry = entry + conv_b_ref[...]
        table[tap * vocab : (tap + 1) * vocab, :] = entry
    full = table[...].T
    high = full.astype(BF16)
    table_hi[...] = high
    table_lo[...] = (full - high.astype(F32)).astype(BF16)


def pooled_features(
    tokens_ref, lengths_ref, inv_len_ref, first, rows, taps, vocab, padded, onehot, table_hi, table_lo, pooled
):
    seq = tokens_ref.shape[1]
    channels = inv_len_ref.shape[0]
    positions = (seq - taps) // 2 + 1
    padded[...] = jnp.zeros_like(padded)
    padded[:, :seq] = tokens_ref[pl.ds(first, rows), :]
    token_rows = padded[...].T
    vocab_ids = lax.broadcasted_iota(jnp.int32, (vocab, rows), 0)
    for spot in range(seq):
        hit = jnp.broadcast_to(token_rows[spot : spot + 1, :], (vocab, rows)) == vocab_ids
        onehot[spot * vocab : (spot + 1) * vocab, :] = jnp.where(hit, 1.0, 0.0).astype(BF16)
    counts = (lengths_ref[:, pl.ds(first, rows)] - taps) // 2 + 1
    pooled[...] = jnp.zeros_like(pooled)
    root = math.sqrt(2.0 / math.pi)

    def position_step(group, carry):
        total = None
        for part in range(GROUP):
            position = group * GROUP + part
            start = pl.multiple_of(position * (2 * vocab), 2 * vocab)
            window = onehot[pl.ds(start, taps * vocab), :]
            preact = jnp.dot(table_hi[...], window, preferred_element_type=F32)
            preact = preact + jnp.dot(table_lo[...], window, preferred_element_type=F32)
            inner = preact * (root + (root * 0.044715) * (preact * preact))
            half = jnp.where(position < counts, 0.5, 0.0)
            weighted = preact * half
            term = weighted + weighted * jnp.tanh(inner)
            total = term if total is None else total + term
        pooled[...] += total
        return carry

    lax.fori_loop(0, positions // GROUP, position_step, 0)
    mean_pool = pooled[...] / counts.astype(F32)
    centered = mean_pool - jnp.mean(mean_pool, axis=0, keepdims=True)
    variance = jnp.mean(centered * centered, axis=0, keepdims=True)
    normed = centered * lax.rsqrt(variance + 1e-05)
    return (normed * inv_len_ref[...]).astype(BF16)


def feature_kernel(
    tokens_ref,
    lengths_ref,
    embed_ref,
    conv_w_ref,
    conv_b_ref,
    inv_len_ref,
    cols_ref,
    rows_ref,
    padded,
    onehot,
    table,
    table_hi,
    table_lo,
    pooled,
):
    rows = cols_ref.shape[1]
    channels = inv_len_ref.shape[0]
    first = pl.multiple_of(lax.axis_index("rep") * rows, rows)
    build_table(embed_ref, conv_w_ref, conv_b_ref, table, table_hi, table_lo)
    feat = pooled_features(
        tokens_ref,
        lengths_ref,
        inv_len_ref,
        first,
        rows,
        conv_w_ref.shape[0],
        embed_ref.shape[0],
        padded,
        onehot,
        table_hi,
        table_lo,
        pooled,
    )
    wide = feat.astype(F32)
    half_sq = -0.5 * jnp.sum(wide * wide, axis=0, keepdims=True)
    cols_ref[:channels, :] = feat
    high = half_sq.astype(BF16).astype(F32)
    middle = (half_sq - high).astype(BF16).astype(F32)
    low = half_sq - high - middle
    order = lax.broadcasted_iota(jnp.int32, (EXTRA, rows), 0)
    tail = jnp.where(order == 0, high, jnp.where(order == 1, middle, jnp.where(order == 2, low, 0.0)))
    cols_ref[channels : channels + EXTRA, :] = tail.astype(BF16)
    rows_ref[...] = wide.T.astype(BF16)


def apply_kernel(
    hyper_ref,
    tokens_ref,
    lengths_ref,
    embed_ref,
    conv_w_ref,
    conv_b_ref,
    inv_len_ref,
    own_ref,
    prev_ref,
    coupling_ref,
    x_ref,
    sums_ref,
    cols_ref,
    rows_ref,
    padded,
    onehot,
    table,
    table_hi,
    table_lo,
    pooled,
    probe_blocks,
    probe_send,
    probe_recv,
    share_send,
    share_recv,
    row_blocks,
    col_blocks,
    row_halves,
    totals,
    partial_out,
    partial_in,
    gram_out,
    gram_in,
    line_in,
    gathered,
    row_send,
    row_recv,
    col_send,
    col_recv,
    side_send,
    side_recv,
    partial_send,
    partial_recv,
    gram_send,
    gram_recv,
    line_send,
    line_recv,
    gather_send,
    gather_recv,
):
    rows, channels = rows_ref.shape
    mates = row_blocks.shape[0]
    line = col_blocks.shape[0]
    plane = gram_out.shape[0]
    width = prev_ref.shape[1]
    reps = lax.axis_size("rep")
    low = plane // reps
    blk = lax.axis_index("blk")
    rep = lax.axis_index("rep")
    core = lax.rem(blk, 2)
    other = 1 - core
    mine = blk // low
    my_plane = lax.rem(blk, low) * reps + rep
    my_mate = (lax.rem(blk, low) // 2) * reps + rep

    def plane_id(spot):
        return {"blk": mine * low + spot // reps, "rep": lax.rem(spot, reps)}

    def mate_id(spot):
        return {"blk": mine * low + (spot // reps) * 2 + core, "rep": lax.rem(spot, reps)}

    def line_id(spot):
        return {"blk": spot * low + lax.rem(blk, low), "rep": rep}

    sibling = {"blk": blk + 1 - 2 * core, "rep": rep}

    def plane_peer(step):
        return lax.rem(my_plane + step, plane)

    def mate_peer(step):
        return lax.rem(my_mate + step, mates)

    line_peers = [mine, mine + 1 - 2 * lax.rem(mine, 2), lax.rem(mine + 2, 4), 3 - mine]

    def copy(src, dst, send_sem, recv_sem, device):
        return pltpu.make_async_remote_copy(
            src_ref=src,
            dst_ref=dst,
            send_sem=send_sem,
            recv_sem=recv_sem,
            device_id=device,
            device_id_type=pl.DeviceIdType.MESH,
        )

    def each_plane_peer(action):
        def body(step, carry):
            action(step, plane_peer(step))
            return carry

        lax.fori_loop(1, plane, body, 0)

    def each_mate(action):
        def body(step, carry):
            action(step, mate_peer(step))
            return carry

        lax.fori_loop(1, mates, body, 0)

    barrier = pltpu.get_barrier_semaphore()

    def greet(step, peer):
        pl.semaphore_signal(barrier, inc=1, device_id=plane_id(peer), device_id_type=pl.DeviceIdType.MESH)

    each_plane_peer(greet)
    for peer in line_peers[1:]:
        pl.semaphore_signal(barrier, inc=1, device_id=line_id(peer), device_id_type=pl.DeviceIdType.MESH)
    own = own_ref[pl.ds(pl.multiple_of(rep * rows, rows), rows), :].astype(F32)
    probe_blocks[core, mine] = own.T.astype(BF16)
    pl.semaphore_wait(barrier, plane - 1 + line - 1)

    def probe_copy(order, slot, peer):
        return copy(
            probe_blocks.at[core, mine],
            probe_blocks.at[core, slot],
            probe_send.at[order],
            probe_recv.at[slot],
            line_id(peer),
        )

    def share_copy(lane):
        return copy(probe_blocks.at[lane], probe_blocks.at[lane], share_send.at[0], share_recv.at[0], sibling)

    for order in range(1, line):
        probe_copy(order, mine, line_peers[order]).start()
    feature_kernel(
        tokens_ref,
        lengths_ref,
        embed_ref,
        conv_w_ref,
        conv_b_ref,
        inv_len_ref,
        cols_ref,
        rows_ref,
        padded,
        onehot,
        table,
        table_hi,
        table_lo,
        pooled,
    )

    def col_copy(order, slot, peer):
        return copy(cols_ref, col_blocks.at[slot, core], col_send.at[order], col_recv.at[slot], line_id(peer))

    def side_copy(slot, lane, src=None):
        src = col_blocks.at[slot, lane] if src is None else src
        return copy(src, col_blocks.at[slot, lane], side_send.at[slot], side_recv.at[slot], sibling)

    def row_copy(step, slot, peer):
        return copy(rows_ref, row_blocks.at[slot], row_send.at[step], row_recv.at[slot], mate_id(peer))

    col_copy(1, mine, line_peers[1]).start()
    each_mate(lambda step, peer: row_copy(step, my_mate, peer).start())
    col_copy(2, mine, line_peers[2]).start()
    col_copy(3, mine, line_peers[3]).start()
    side_copy(mine, core, cols_ref).start()
    row_blocks[my_mate] = rows_ref[...]
    col_blocks[mine, core] = cols_ref[...]
    amplitude = hyper_ref[0]
    for order in range(1, line):
        probe_copy(order, line_peers[order], line_peers[order]).wait_recv()
    share_copy(core).start()
    root = 1.0 / math.sqrt(rows * plane * line)
    coupled = lax.dot_general(
        prev_ref[...].astype(F32),
        coupling_ref[...],
        (((1,), (1,)), ((), ())),
        precision=HIGH,
        preferred_element_type=F32,
    )
    x_ref[:, :width] = own * root
    x_ref[:, width:] = (hyper_ref[1] * own - coupled) * root
    share_copy(other).wait_recv()

    def partial_copy(step, slot, peer):
        return copy(
            partial_out.at[step], partial_in.at[slot], partial_send.at[step], partial_recv.at[slot], mate_id(peer)
        )

    def packed(value):
        return jnp.concatenate([value[: rows // 2, :], value[rows // 2 :, :]], axis=1)

    def column_pass(source, lane, first, last):
        cols = col_blocks.at[source, lane]
        col_half = jnp.sum(cols[channels : channels + EXTRA, :].astype(F32), axis=0, keepdims=True)
        block_probes = probe_blocks[lane, source].astype(F32).T.astype(BF16)
        group = 1 if first else 2 if last else 4

        def group_step(index, carry):
            steps = [group * index + part + (1 if last else 0) for part in range(group)]
            if first:
                for step in steps:
                    spot = mate_peer(step)

                    @pl.when(step > 0)
                    def _():
                        row_copy(step, spot, spot).wait_recv()

                    wide = row_blocks[spot].astype(F32)
                    row_halves[spot] = -0.5 * jnp.sum(wide * wide, axis=1, keepdims=True)
            values = []
            for step in steps:
                spot = mate_peer(step)
                inner = jnp.dot(row_blocks[spot], cols[:channels, :], preferred_element_type=F32)
                exponent = jnp.minimum(inner + (row_halves[spot] + col_half), 0.0)
                weights = (amplitude * jnp.exp(exponent)).astype(BF16)
                value = jnp.dot(weights, block_probes, preferred_element_type=F32)
                values.append(value if first else value + totals[spot])
            for step, value in zip(steps, values):
                spot = mate_peer(step)
                if not last:
                    totals[spot] = value
                    continue
                partial_out[step] = packed(value)

                @pl.when(step < mates)
                def _():
                    partial_copy(step, my_mate, spot).start()

            return carry

        lax.fori_loop(0, mates // group, group_step, 0)

    for order in range(line):
        source = line_peers[order]
        if order:
            col_copy(order, source, source).wait_recv()
            side_copy(source, core).start()
        column_pass(source, core, order == 0, False)
        side_copy(source, other).wait_recv()
        column_pass(source, other, False, order == line - 1)

    def add_partial(step, total):
        spot = mate_peer(step)
        partial_copy(step, spot, spot).wait_recv()
        return total + partial_in[spot]

    total = lax.fori_loop(1, mates, add_partial, partial_out[mates])
    applied = jnp.concatenate([total[:, :width], total[:, width:]], axis=0)
    x_ref[:, width:] += applied * root
    both = x_ref[...]
    gram = jnp.dot(both.T, both, precision=HIGH, preferred_element_type=F32)
    piece = gram_out.shape[1]
    for spot in range(plane):
        gram_out[spot] = gram[spot * piece : (spot + 1) * piece, :]

    def gram_copy(step, target, slot):
        return copy(gram_out.at[target], gram_in.at[slot], gram_send.at[step], gram_recv.at[slot], plane_id(target))

    each_plane_peer(lambda step, peer: gram_copy(step, peer, my_plane).start())

    def add_gram(step, total):
        spot = plane_peer(step)
        gram_copy(step, spot, spot).wait_recv()
        return total + gram_in[spot]

    line_in[mine] = lax.fori_loop(1, plane, add_gram, gram_out[my_plane])

    def line_copy(order, slot, peer):
        return copy(line_in.at[mine], line_in.at[slot], line_send.at[order], line_recv.at[slot], line_id(peer))

    for order in range(1, line):
        line_copy(order, mine, line_peers[order]).start()
    for order in range(1, line):
        line_copy(order, line_peers[order], line_peers[order]).wait_recv()
    gathered[my_plane] = (line_in[0] + line_in[1]) + (line_in[2] + line_in[3])

    def gather_copy(step, slot, peer):
        return copy(
            gathered.at[my_plane], gathered.at[slot], gather_send.at[step], gather_recv.at[slot], plane_id(peer)
        )

    each_plane_peer(lambda step, peer: gather_copy(step, my_plane, peer).start())
    each_plane_peer(lambda step, peer: gather_copy(step, peer, peer).wait_recv())
    for spot in range(plane):
        sums_ref[spot * piece : (spot + 1) * piece, :] = gathered[spot]
    for order in range(1, line):
        line_copy(order, mine, line_peers[order]).wait_send()
        col_copy(order, mine, line_peers[order]).wait_send()
        probe_copy(order, mine, line_peers[order]).wait_send()
    share_copy(core).wait_send()
    for slot in range(line):
        side_copy(slot, core).wait_send()

    def drain_mate(step, peer):
        row_copy(step, my_mate, peer).wait_send()
        partial_copy(step, my_mate, peer).wait_send()

    def drain(step, peer):
        gram_copy(step, peer, my_plane).wait_send()
        gather_copy(step, my_plane, peer).wait_send()

    each_mate(drain_mate)
    each_plane_peer(drain)


def finish_kernel(root, x_ref, sums_ref, a_ref, r_ref, next_ref):
    width = a_ref.shape[0]
    corr = sums_ref[:width, :width]
    block_a = sums_ref[:width, width:]
    cross = sums_ref[width:, width:]
    a_ref[...] = block_a
    resid = x_ref[:, width:] - jnp.dot(x_ref[:, :width], block_a, precision=HIGH, preferred_element_type=F32)
    middle = jnp.dot(corr, block_a, precision=HIGH, preferred_element_type=F32) - 2.0 * block_a
    gram = cross + jnp.dot(block_a.T, middle, precision=HIGH, preferred_element_type=F32)
    row = lax.broadcasted_iota(jnp.int32, (width, width), 0)
    col = lax.broadcasted_iota(jnp.int32, (width, width), 1)
    eye = jnp.where(row == col, 1.0, 0.0)
    work = jnp.concatenate([gram, eye], axis=1)
    done = []
    for base in range(0, width, PANEL):
        lines = [work[base + i : base + i + 1, :] for i in range(PANEL)]
        sides = [jnp.broadcast_to(work[:, base + i : base + i + 1], work.shape) for i in range(PANEL)]
        pivots = {
            (i, k): jnp.broadcast_to(lines[i][:, base + k : base + k + 1], lines[i].shape)
            for i in range(PANEL)
            for k in range(i, PANEL)
        }
        change = None
        for i in range(PANEL):
            scale = lax.rsqrt(pivots[i, i])
            line = lines[i] * scale
            side = sides[i] * scale
            done.append(line)
            beta = {k: pivots[i, k] * scale for k in range(i + 1, PANEL)}
            for k in range(i + 1, PANEL):
                lines[k] = lines[k] - beta[k] * line
                sides[k] = sides[k] - beta[k] * side
                for m in range(k, PANEL):
                    pivots[k, m] = pivots[k, m] - beta[k] * beta[m]
            change = side * line if change is None else change + side * line
        work = work - change
    factor = jnp.concatenate(done, axis=0)
    r_ref[...] = jnp.where(row <= col, factor[:, :width], 0.0)
    inverse = factor[:, width:].T
    next_ref[...] = jnp.dot(resid, inverse, precision=HIGH, preferred_element_type=F32) * root


VMEM = pl.BlockSpec(memory_space=pltpu.VMEM)
SMEM = pl.BlockSpec(memory_space=pltpu.SMEM)
PARAMS = pltpu.CompilerParams(vmem_limit_bytes=48 * 1024 * 1024)


def per_device(tokens, lengths, embed, conv_w, conv_b, inv_len, hyper, probes, prev_probes, coupling):
    rows, width = prev_probes.shape
    vocab, channels = embed.shape
    taps = conv_w.shape[0]
    seq = tokens.shape[1]
    depth = taps * vocab
    line = LINE
    plane = lax.axis_size("blk") // line * lax.axis_size("rep")
    mates = plane // 2
    piece = 2 * width // plane
    dma = pltpu.SemaphoreType.DMA
    pair, sums = pl.pallas_call(
        apply_kernel,
        out_shape=(
            jax.ShapeDtypeStruct((rows, 2 * width), F32),
            jax.ShapeDtypeStruct((2 * width, 2 * width), F32),
        ),
        in_specs=[SMEM] + [VMEM] * 9,
        out_specs=(VMEM, VMEM),
        scratch_shapes=[
            pltpu.VMEM((channels + EXTRA, rows), BF16),
            pltpu.VMEM((rows, channels), BF16),
            pltpu.VMEM((rows, 128), jnp.int32),
            pltpu.VMEM((seq * vocab, rows), BF16),
            pltpu.VMEM((depth, channels), F32),
            pltpu.VMEM((channels, depth), BF16),
            pltpu.VMEM((channels, depth), BF16),
            pltpu.VMEM((channels, rows), F32),
            pltpu.VMEM((2, line, width, rows), BF16),
            dma((line,)),
            dma((line,)),
            dma((1,)),
            dma((1,)),
            pltpu.VMEM((mates, rows, channels), BF16),
            pltpu.VMEM((line, 2, channels + EXTRA, rows), BF16),
            pltpu.VMEM((mates, rows, 1), F32),
            pltpu.VMEM((mates, rows, width), F32),
            pltpu.VMEM((mates + 1, rows // 2, 2 * width), F32),
            pltpu.VMEM((mates, rows // 2, 2 * width), F32),
            pltpu.VMEM((plane, piece, 2 * width), F32),
            pltpu.VMEM((plane, piece, 2 * width), F32),
            pltpu.VMEM((line, piece, 2 * width), F32),
            pltpu.VMEM((plane, piece, 2 * width), F32),
            dma((mates,)),
            dma((mates,)),
            dma((line,)),
            dma((line,)),
            dma((line,)),
            dma((line,)),
            dma((mates,)),
            dma((mates,)),
            dma((plane,)),
            dma((plane,)),
            dma((line,)),
            dma((line,)),
            dma((plane,)),
            dma((plane,)),
        ],
        compiler_params=pltpu.CompilerParams(
            vmem_limit_bytes=48 * 1024 * 1024, collective_id=0, has_side_effects=True
        ),
    )(
        hyper,
        tokens,
        lengths.reshape(1, -1),
        embed,
        conv_w,
        conv_b.reshape(1, -1),
        inv_len.reshape(-1, 1),
        probes,
        prev_probes,
        coupling,
    )
    root = math.sqrt(rows * plane * line)
    return pl.pallas_call(
        functools.partial(finish_kernel, root),
        out_shape=(
            jax.ShapeDtypeStruct((width, width), F32),
            jax.ShapeDtypeStruct((width, width), F32),
            jax.ShapeDtypeStruct((rows, width), F32),
        ),
        in_specs=[VMEM] * 2,
        out_specs=(VMEM, VMEM, VMEM),
        compiler_params=PARAMS,
    )(pair, sums)


def solution(mesh):
    return jax.shard_map(
        per_device,
        mesh=mesh,
        in_specs=(
            P("blk", None),
            P("blk"),
            P(),
            P(),
            P(),
            P(),
            P(),
            P("blk", None),
            P(("blk", "rep"), None),
            P(),
        ),
        out_specs=(P(), P(), P(("blk", "rep"), None)),
        check_vma=False,
    )
```

```python
import functools
import math

import jax
import jax.numpy as jnp
from jax import lax
from jax.experimental import pallas as pl
from jax.experimental.pallas import tpu as pltpu
from jax.sharding import PartitionSpec as P

F32 = jnp.float32
BF16 = jnp.bfloat16
EXTRA = 16
LINE = 4
GROUP = 8
PANEL = 8
HIGH = lax.Precision.HIGHEST


def build_table(embed_ref, conv_w_ref, conv_b_ref, table, table_hi, table_lo):
    taps, width, channels = conv_w_ref.shape
    vocab = embed_ref.shape[0]
    groups = channels // width
    in_group = lax.broadcasted_iota(jnp.int32, (channels, channels), 0) // width
    out_group = lax.broadcasted_iota(jnp.int32, (channels, channels), 1) // width
    same = in_group == out_group
    for tap in range(taps):
        tiled = jnp.concatenate([conv_w_ref[tap].astype(F32)] * groups, axis=0)
        dense = jnp.where(same, tiled, 0.0).astype(BF16)
        entry = jnp.dot(embed_ref[...], dense, preferred_element_type=F32)
        if tap == 0:
            entry = entry + conv_b_ref[...]
        table[tap * vocab : (tap + 1) * vocab, :] = entry
    full = table[...].T
    high = full.astype(BF16)
    table_hi[...] = high
    table_lo[...] = (full - high.astype(F32)).astype(BF16)


def pooled_features(
    tokens_ref, lengths_ref, inv_len_ref, first, rows, taps, vocab, padded, onehot, table_hi, table_lo, pooled
):
    seq = tokens_ref.shape[1]
    channels = inv_len_ref.shape[0]
    positions = (seq - taps) // 2 + 1
    padded[...] = jnp.zeros_like(padded)
    padded[:, :seq] = tokens_ref[pl.ds(first, rows), :]
    token_rows = padded[...].T
    vocab_ids = lax.broadcasted_iota(jnp.int32, (vocab, rows), 0)
    for spot in range(seq):
        hit = jnp.broadcast_to(token_rows[spot : spot + 1, :], (vocab, rows)) == vocab_ids
        onehot[spot * vocab : (spot + 1) * vocab, :] = jnp.where(hit, 1.0, 0.0).astype(BF16)
    counts = (lengths_ref[:, pl.ds(first, rows)] - taps) // 2 + 1
    pooled[...] = jnp.zeros_like(pooled)
    root = math.sqrt(2.0 / math.pi)

    def position_step(group, carry):
        total = None
        for part in range(GROUP):
            position = group * GROUP + part
            start = pl.multiple_of(position * (2 * vocab), 2 * vocab)
            window = onehot[pl.ds(start, taps * vocab), :]
            preact = jnp.dot(table_hi[...], window, preferred_element_type=F32)
            preact = preact + jnp.dot(table_lo[...], window, preferred_element_type=F32)
            inner = preact * (root + (root * 0.044715) * (preact * preact))
            half = jnp.where(position < counts, 0.5, 0.0)
            weighted = preact * half
            term = weighted + weighted * jnp.tanh(inner)
            total = term if total is None else total + term
        pooled[...] += total
        return carry

    lax.fori_loop(0, positions // GROUP, position_step, 0)
    mean_pool = pooled[...] / counts.astype(F32)
    centered = mean_pool - jnp.mean(mean_pool, axis=0, keepdims=True)
    variance = jnp.mean(centered * centered, axis=0, keepdims=True)
    normed = centered * lax.rsqrt(variance + 1e-05)
    return (normed * inv_len_ref[...]).astype(BF16)


def feature_kernel(
    tokens_ref,
    lengths_ref,
    embed_ref,
    conv_w_ref,
    conv_b_ref,
    inv_len_ref,
    cols_ref,
    rows_ref,
    padded,
    onehot,
    table,
    table_hi,
    table_lo,
    pooled,
):
    rows = cols_ref.shape[1]
    channels = inv_len_ref.shape[0]
    first = pl.multiple_of(lax.axis_index("rep") * rows, rows)
    build_table(embed_ref, conv_w_ref, conv_b_ref, table, table_hi, table_lo)
    feat = pooled_features(
        tokens_ref,
        lengths_ref,
        inv_len_ref,
        first,
        rows,
        conv_w_ref.shape[0],
        embed_ref.shape[0],
        padded,
        onehot,
        table_hi,
        table_lo,
        pooled,
    )
    wide = feat.astype(F32)
    half_sq = -0.5 * jnp.sum(wide * wide, axis=0, keepdims=True)
    cols_ref[:channels, :] = feat
    high = half_sq.astype(BF16).astype(F32)
    middle = (half_sq - high).astype(BF16).astype(F32)
    low = half_sq - high - middle
    order = lax.broadcasted_iota(jnp.int32, (EXTRA, rows), 0)
    tail = jnp.where(order == 0, high, jnp.where(order == 1, middle, jnp.where(order == 2, low, 0.0)))
    cols_ref[channels : channels + EXTRA, :] = tail.astype(BF16)
    rows_ref[...] = wide.T.astype(BF16)


def apply_kernel(
    hyper_ref,
    tokens_ref,
    lengths_ref,
    embed_ref,
    conv_w_ref,
    conv_b_ref,
    inv_len_ref,
    own_ref,
    prev_ref,
    coupling_ref,
    x_ref,
    sums_ref,
    cols_ref,
    rows_ref,
    padded,
    onehot,
    table,
    table_hi,
    table_lo,
    pooled,
    probe_blocks,
    probe_send,
    probe_recv,
    share_send,
    share_recv,
    row_blocks,
    col_blocks,
    row_halves,
    totals,
    partial_out,
    partial_in,
    gram_out,
    gram_in,
    line_in,
    gathered,
    row_send,
    row_recv,
    col_send,
    col_recv,
    side_send,
    side_recv,
    partial_send,
    partial_recv,
    gram_send,
    gram_recv,
    line_send,
    line_recv,
    gather_send,
    gather_recv,
):
    rows, channels = rows_ref.shape
    mates = row_blocks.shape[0]
    line = col_blocks.shape[0]
    plane = gram_out.shape[0]
    width = prev_ref.shape[1]
    reps = lax.axis_size("rep")
    low = plane // reps
    blk = lax.axis_index("blk")
    rep = lax.axis_index("rep")
    core = lax.rem(blk, 2)
    other = 1 - core
    mine = blk // low
    my_plane = lax.rem(blk, low) * reps + rep
    my_mate = (lax.rem(blk, low) // 2) * reps + rep

    def plane_id(spot):
        return {"blk": mine * low + spot // reps, "rep": lax.rem(spot, reps)}

    def mate_id(spot):
        return {"blk": mine * low + (spot // reps) * 2 + core, "rep": lax.rem(spot, reps)}

    def line_id(spot):
        return {"blk": spot * low + lax.rem(blk, low), "rep": rep}

    sibling = {"blk": blk + 1 - 2 * core, "rep": rep}

    def plane_peer(step):
        return lax.rem(my_plane + step, plane)

    def mate_peer(step):
        return lax.rem(my_mate + step, mates)

    line_peers = [mine, mine + 1 - 2 * lax.rem(mine, 2), lax.rem(mine + 2, 4), 3 - mine]

    def copy(src, dst, send_sem, recv_sem, device):
        return pltpu.make_async_remote_copy(
            src_ref=src,
            dst_ref=dst,
            send_sem=send_sem,
            recv_sem=recv_sem,
            device_id=device,
            device_id_type=pl.DeviceIdType.MESH,
        )

    def each_plane_peer(action):
        def body(step, carry):
            action(step, plane_peer(step))
            return carry

        lax.fori_loop(1, plane, body, 0)

    def each_mate(action):
        def body(step, carry):
            action(step, mate_peer(step))
            return carry

        lax.fori_loop(1, mates, body, 0)

    barrier = pltpu.get_barrier_semaphore()

    def greet(step, peer):
        pl.semaphore_signal(barrier, inc=1, device_id=plane_id(peer), device_id_type=pl.DeviceIdType.MESH)

    each_plane_peer(greet)
    for peer in line_peers[1:]:
        pl.semaphore_signal(barrier, inc=1, device_id=line_id(peer), device_id_type=pl.DeviceIdType.MESH)
    own = own_ref[pl.ds(pl.multiple_of(rep * rows, rows), rows), :].astype(F32)
    probe_blocks[core, mine] = own.T.astype(BF16)
    pl.semaphore_wait(barrier, plane - 1 + line - 1)

    def probe_copy(order, slot, peer):
        return copy(
            probe_blocks.at[core, mine],
            probe_blocks.at[core, slot],
            probe_send.at[order],
            probe_recv.at[slot],
            line_id(peer),
        )

    def share_copy(lane):
        return copy(probe_blocks.at[lane], probe_blocks.at[lane], share_send.at[0], share_recv.at[0], sibling)

    for order in range(1, line):
        probe_copy(order, mine, line_peers[order]).start()
    feature_kernel(
        tokens_ref,
        lengths_ref,
        embed_ref,
        conv_w_ref,
        conv_b_ref,
        inv_len_ref,
        cols_ref,
        rows_ref,
        padded,
        onehot,
        table,
        table_hi,
        table_lo,
        pooled,
    )

    def col_copy(order, slot, peer):
        return copy(cols_ref, col_blocks.at[slot, core], col_send.at[order], col_recv.at[slot], line_id(peer))

    def side_copy(slot, lane, src=None):
        src = col_blocks.at[slot, lane] if src is None else src
        return copy(src, col_blocks.at[slot, lane], side_send.at[slot], side_recv.at[slot], sibling)

    def row_copy(step, slot, peer):
        return copy(rows_ref, row_blocks.at[slot], row_send.at[step], row_recv.at[slot], mate_id(peer))

    col_copy(1, mine, line_peers[1]).start()
    each_mate(lambda step, peer: row_copy(step, my_mate, peer).start())
    col_copy(2, mine, line_peers[2]).start()
    col_copy(3, mine, line_peers[3]).start()
    side_copy(mine, core, cols_ref).start()
    row_blocks[my_mate] = rows_ref[...]
    col_blocks[mine, core] = cols_ref[...]
    amplitude = hyper_ref[0]
    for order in range(1, line):
        probe_copy(order, line_peers[order], line_peers[order]).wait_recv()
    share_copy(core).start()
    root = 1.0 / math.sqrt(rows * plane * line)
    coupled = lax.dot_general(
        prev_ref[...].astype(F32),
        coupling_ref[...],
        (((1,), (1,)), ((), ())),
        precision=HIGH,
        preferred_element_type=F32,
    )
    x_ref[:, :width] = own * root
    x_ref[:, width:] = (hyper_ref[1] * own - coupled) * root
    share_copy(other).wait_recv()

    def partial_copy(step, slot, peer):
        return copy(
            partial_out.at[step], partial_in.at[slot], partial_send.at[step], partial_recv.at[slot], mate_id(peer)
        )

    def packed(value):
        return jnp.concatenate([value[: rows // 2, :], value[rows // 2 :, :]], axis=1)

    def column_pass(source, lane, first, last):
        cols = col_blocks.at[source, lane]
        col_half = jnp.sum(cols[channels : channels + EXTRA, :].astype(F32), axis=0, keepdims=True)
        block_probes = probe_blocks[lane, source].astype(F32).T.astype(BF16)
        group = 1 if first else 2 if last else 4

        def group_step(index, carry):
            steps = [group * index + part + (1 if last else 0) for part in range(group)]
            if first:
                for step in steps:
                    spot = mate_peer(step)

                    @pl.when(step > 0)
                    def _():
                        row_copy(step, spot, spot).wait_recv()

                    wide = row_blocks[spot].astype(F32)
                    row_halves[spot] = -0.5 * jnp.sum(wide * wide, axis=1, keepdims=True)
            values = []
            for step in steps:
                spot = mate_peer(step)
                inner = jnp.dot(row_blocks[spot], cols[:channels, :], preferred_element_type=F32)
                exponent = jnp.minimum(inner + (row_halves[spot] + col_half), 0.0)
                weights = (amplitude * jnp.exp(exponent)).astype(BF16)
                value = jnp.dot(weights, block_probes, preferred_element_type=F32)
                values.append(value if first else value + totals[spot])
            for step, value in zip(steps, values):
                spot = mate_peer(step)
                if not last:
                    totals[spot] = value
                    continue
                partial_out[step] = packed(value)

                @pl.when(step < mates)
                def _():
                    partial_copy(step, my_mate, spot).start()

            return carry

        lax.fori_loop(0, mates // group, group_step, 0)

    for order in range(line):
        source = line_peers[order]
        if order:
            col_copy(order, source, source).wait_recv()
            side_copy(source, core).start()
        column_pass(source, core, order == 0, False)
        side_copy(source, other).wait_recv()
        column_pass(source, other, False, order == line - 1)

    def add_partial(step, total):
        spot = mate_peer(step)
        partial_copy(step, spot, spot).wait_recv()
        return total + partial_in[spot]

    total = lax.fori_loop(1, mates, add_partial, partial_out[mates])
    applied = jnp.concatenate([total[:, :width], total[:, width:]], axis=0)
    x_ref[:, width:] += applied * root
    both = x_ref[...]
    gram = jnp.dot(both.T, both, precision=HIGH, preferred_element_type=F32)
    piece = gram_out.shape[1]
    for spot in range(plane):
        gram_out[spot] = gram[spot * piece : (spot + 1) * piece, :]

    def gram_copy(step, target, slot):
        return copy(gram_out.at[target], gram_in.at[slot], gram_send.at[step], gram_recv.at[slot], plane_id(target))

    each_plane_peer(lambda step, peer: gram_copy(step, peer, my_plane).start())

    def add_gram(step, total):
        spot = plane_peer(step)
        gram_copy(step, spot, spot).wait_recv()
        return total + gram_in[spot]

    line_in[mine] = lax.fori_loop(1, plane, add_gram, gram_out[my_plane])

    def line_copy(order, slot, peer):
        return copy(line_in.at[mine], line_in.at[slot], line_send.at[order], line_recv.at[slot], line_id(peer))

    for order in range(1, line):
        line_copy(order, mine, line_peers[order]).start()
    for order in range(1, line):
        line_copy(order, line_peers[order], line_peers[order]).wait_recv()
    gathered[my_plane] = (line_in[0] + line_in[1]) + (line_in[2] + line_in[3])

    def gather_copy(step, slot, peer):
        return copy(
            gathered.at[my_plane], gathered.at[slot], gather_send.at[step], gather_recv.at[slot], plane_id(peer)
        )

    each_plane_peer(lambda step, peer: gather_copy(step, my_plane, peer).start())
    each_plane_peer(lambda step, peer: gather_copy(step, peer, peer).wait_recv())
    for spot in range(plane):
        sums_ref[spot * piece : (spot + 1) * piece, :] = gathered[spot]
    for order in range(1, line):
        line_copy(order, mine, line_peers[order]).wait_send()
        col_copy(order, mine, line_peers[order]).wait_send()
        probe_copy(order, mine, line_peers[order]).wait_send()
    share_copy(core).wait_send()
    for slot in range(line):
        side_copy(slot, core).wait_send()

    def drain_mate(step, peer):
        row_copy(step, my_mate, peer).wait_send()
        partial_copy(step, my_mate, peer).wait_send()

    def drain(step, peer):
        gram_copy(step, peer, my_plane).wait_send()
        gather_copy(step, my_plane, peer).wait_send()

    each_mate(drain_mate)
    each_plane_peer(drain)


def finish_kernel(root, x_ref, sums_ref, a_ref, r_ref, next_ref):
    width = a_ref.shape[0]
    corr = sums_ref[:width, :width]
    block_a = sums_ref[:width, width:]
    cross = sums_ref[width:, width:]
    a_ref[...] = block_a
    resid = x_ref[:, width:] - jnp.dot(x_ref[:, :width], block_a, precision=HIGH, preferred_element_type=F32)
    middle = jnp.dot(corr, block_a, precision=HIGH, preferred_element_type=F32) - 2.0 * block_a
    gram = cross + jnp.dot(block_a.T, middle, precision=HIGH, preferred_element_type=F32)
    row = lax.broadcasted_iota(jnp.int32, (width, width), 0)
    col = lax.broadcasted_iota(jnp.int32, (width, width), 1)
    eye = jnp.where(row == col, 1.0, 0.0)
    work = jnp.concatenate([gram, eye], axis=1)
    done = []
    for base in range(0, width, PANEL):
        lines = [work[base + i : base + i + 1, :] for i in range(PANEL)]
        sides = [jnp.broadcast_to(work[:, base + i : base + i + 1], work.shape) for i in range(PANEL)]
        pivots = {
            (i, k): jnp.broadcast_to(lines[i][:, base + k : base + k + 1], lines[i].shape)
            for i in range(PANEL)
            for k in range(i, PANEL)
        }
        change = None
        for i in range(PANEL):
            scale = lax.rsqrt(pivots[i, i])
            line = lines[i] * scale
            side = sides[i] * scale
            done.append(line)
            beta = {k: pivots[i, k] * scale for k in range(i + 1, PANEL)}
            for k in range(i + 1, PANEL):
                lines[k] = lines[k] - beta[k] * line
                sides[k] = sides[k] - beta[k] * side
                for m in range(k, PANEL):
                    pivots[k, m] = pivots[k, m] - beta[k] * beta[m]
            change = side * line if change is None else change + side * line
        work = work - change
    factor = jnp.concatenate(done, axis=0)
    r_ref[...] = jnp.where(row <= col, factor[:, :width], 0.0)
    inverse = factor[:, width:].T
    next_ref[...] = jnp.dot(resid, inverse, precision=HIGH, preferred_element_type=F32) * root


VMEM = pl.BlockSpec(memory_space=pltpu.VMEM)
SMEM = pl.BlockSpec(memory_space=pltpu.SMEM)
PARAMS = pltpu.CompilerParams(vmem_limit_bytes=48 * 1024 * 1024)


def per_device(tokens, lengths, embed, conv_w, conv_b, inv_len, hyper, probes, prev_probes, coupling):
    rows, width = prev_probes.shape
    vocab, channels = embed.shape
    taps = conv_w.shape[0]
    seq = tokens.shape[1]
    depth = taps * vocab
    line = LINE
    plane = lax.axis_size("blk") // line * lax.axis_size("rep")
    mates = plane // 2
    piece = 2 * width // plane
    dma = pltpu.SemaphoreType.DMA
    pair, sums = pl.pallas_call(
        apply_kernel,
        out_shape=(
            jax.ShapeDtypeStruct((rows, 2 * width), F32),
            jax.ShapeDtypeStruct((2 * width, 2 * width), F32),
        ),
        in_specs=[SMEM] + [VMEM] * 9,
        out_specs=(VMEM, VMEM),
        scratch_shapes=[
            pltpu.VMEM((channels + EXTRA, rows), BF16),
            pltpu.VMEM((rows, channels), BF16),
            pltpu.VMEM((rows, 128), jnp.int32),
            pltpu.VMEM((seq * vocab, rows), BF16),
            pltpu.VMEM((depth, channels), F32),
            pltpu.VMEM((channels, depth), BF16),
            pltpu.VMEM((channels, depth), BF16),
            pltpu.VMEM((channels, rows), F32),
            pltpu.VMEM((2, line, width, rows), BF16),
            dma((line,)),
            dma((line,)),
            dma((1,)),
            dma((1,)),
            pltpu.VMEM((mates, rows, channels), BF16),
            pltpu.VMEM((line, 2, channels + EXTRA, rows), BF16),
            pltpu.VMEM((mates, rows, 1), F32),
            pltpu.VMEM((mates, rows, width), F32),
            pltpu.VMEM((mates + 1, rows // 2, 2 * width), F32),
            pltpu.VMEM((mates, rows // 2, 2 * width), F32),
            pltpu.VMEM((plane, piece, 2 * width), F32),
            pltpu.VMEM((plane, piece, 2 * width), F32),
            pltpu.VMEM((line, piece, 2 * width), F32),
            pltpu.VMEM((plane, piece, 2 * width), F32),
            dma((mates,)),
            dma((mates,)),
            dma((line,)),
            dma((line,)),
            dma((line,)),
            dma((line,)),
            dma((mates,)),
            dma((mates,)),
            dma((plane,)),
            dma((plane,)),
            dma((line,)),
            dma((line,)),
            dma((plane,)),
            dma((plane,)),
        ],
        compiler_params=pltpu.CompilerParams(
            vmem_limit_bytes=48 * 1024 * 1024, collective_id=0, has_side_effects=True
        ),
    )(
        hyper,
        tokens,
        lengths.reshape(1, -1),
        embed,
        conv_w,
        conv_b.reshape(1, -1),
        inv_len.reshape(-1, 1),
        probes,
        prev_probes,
        coupling,
    )
    root = math.sqrt(rows * plane * line)
    return pl.pallas_call(
        functools.partial(finish_kernel, root),
        out_shape=(
            jax.ShapeDtypeStruct((width, width), F32),
            jax.ShapeDtypeStruct((width, width), F32),
            jax.ShapeDtypeStruct((rows, width), F32),
        ),
        in_specs=[VMEM] * 2,
        out_specs=(VMEM, VMEM, VMEM),
        compiler_params=PARAMS,
    )(pair, sums)


def solution(mesh):
    return jax.shard_map(
        per_device,
        mesh=mesh,
        in_specs=(
            P("blk", None),
            P("blk"),
            P(),
            P(),
            P(),
            P(),
            P(),
            P("blk", None),
            P(("blk", "rep"), None),
            P(),
        ),
        out_specs=(P(), P(), P(("blk", "rep"), None)),
        check_vma=False,
    )
```
